1024 devices in a mesh: grp: 2 (over x_hi), rep: 64 (over z, x_lo), tp: 8 (over y, core).
Axes of the slice: x: 4 (x_hi: 2, x_lo: 2; x = x_hi * 2 + x_lo), y: 4, z: 32, core: 2. Of those that a mesh axis runs over, the one named last changes fastest.
Arguments:
- grad_parts: float32 [8, 5120, 2048], P('tp', ('grp', 'rep')), may hold values from -124 to 124
- master: float32 [5120, 2048], P(('grp', 'rep'), 'tp'), may hold values from -0.078125 to 0.078125
- moment_one: float32 [5120, 2048], P(('grp', 'rep'), 'tp'), may hold values from -1.5 to 1.5
- moment_two: float32 [5120, 2048], P(('grp', 'rep'), 'tp'), may hold values from 0.003 to 0.03
- hidden_in: bfloat16 [512, 4, 5120], P(('grp', 'rep')), may hold values from -6 to 6
- queries: bfloat16 [512, 4, 5120], P(('grp', 'rep'), None, 'tp'), may hold values from -8 to 8
- cache_keys: bfloat16 [512, 1024, 1024], P(('grp', 'rep'), None, 'tp'), may hold values from -8 to 8
- cache_values: bfloat16 [512, 1024, 1024], P(('grp', 'rep'), None, 'tp'), may hold values from -6 to 6
- cache_lengths: int32 [512], P(('grp', 'rep')), may hold values from 16 to 1024
Outputs:
- new_moment_one: float32 [5120, 2048], P(('grp', 'rep'), 'tp')
- new_moment_two: float32 [5120, 2048], P(('grp', 'rep'), 'tp')
- new_entries: bfloat16 [512, 4, 2048], P(('grp', 'rep'), None, 'tp')
- attended: bfloat16 [512, 4, 5120], P(('grp', 'rep'), None, 'tp')
The draws below stay inside these ranges and needn't reach their ends.
Inputs may be any that keep to these rules, and one draw needn't show every extreme that they name: `cache_lengths`: cache slots at or after a row's length hold no part of its cache.
All inputs are finite; a program needn't handle non-finite values.
Results may differ from the reference program's by a relative error of at most 0.0051.
Values may be sent and summed in bfloat16 or wider, within the bound.
No kernel may reach another device: no remote copies, remote signals or barrier semaphores. Data moves between devices by JAX's collectives and lax.ppermute only.
A program may use at most 32 MiB of HBM per device.

```python
import math
import jax
import jax.numpy as jnp
from jax import lax

D = 5120
QH = 40
KVH = 8
HD = 128
CACHE = 1024
STEPS = 4
ROWS = 512
N_GRP = 2
N_REP = 64
N_TP = 8


def grad_levels(key):
    block_rows = D // (N_GRP * N_REP)
    row_power = jax.random.uniform(jax.random.fold_in(key, 34), (N_GRP * N_REP,), jnp.float32, -0.5, 0.0)
    row_level = jnp.repeat(jnp.exp(math.log(10.0) * row_power), block_rows)
    col_power = jax.random.uniform(jax.random.fold_in(key, 35), (2 * KVH,), jnp.float32, -1.0, 0.0)
    col_level = jnp.repeat(jnp.exp(math.log(10.0) * col_power), HD)
    return row_level[None, :, None] * col_level[None, None, :]


def draw_grad_parts(key, part):
    data_index = jnp.arange(N_TP, dtype=jnp.float32)
    row_index = jnp.arange(D, dtype=jnp.float32)
    growth = (1.0 + 2.0 * data_index / (N_TP - 1))[:, None, None] * (1.0 + 2.0 * row_index / (D - 1))[None, :, None]
    growth = growth * grad_levels(key)
    shape = (N_TP, D, 2 * KVH * HD)
    noise = jax.random.truncated_normal(jax.random.fold_in(key, 33), -6.0, 6.0, shape, jnp.float32)
    return noise * growth


def draw_queries(key, part):
    shape = (ROWS, STEPS, QH * HD)
    return jax.random.truncated_normal(jax.random.fold_in(key, 42), -6.0, 6.0, shape, jnp.float32).astype(jnp.bfloat16)


def draw_cache_keys(key, part):
    shape = (ROWS, CACHE, KVH * HD)
    return jax.random.truncated_normal(jax.random.fold_in(key, 52), -6.0, 6.0, shape, jnp.float32).astype(jnp.bfloat16)


def plant(values, key, smallest, top_value):
    longest = values.shape.index(max(values.shape))
    spots = []
    for shift in (0, 1):
        where = [jax.random.randint(jax.random.fold_in(key, axis), (), 0, length) for axis, length in enumerate(values.shape)]
        where[longest] = (where[longest] + shift) % values.shape[longest]
        spots.append(tuple(where))
    return values.at[spots[0]].set(smallest).at[spots[1]].set(top_value)


def block_scale(stream_key, shape, cuts, least, largest):
    gain, own = 1.0, jax.random.fold_in(stream_key, 6)
    for position, parts in cuts:
        draws = jnp.exp(jax.random.uniform(jax.random.fold_in(own, position), (parts,), jnp.float32, least / len(cuts), largest / len(cuts)))
        gain = gain * jnp.repeat(draws, shape[position] // parts).reshape([-1 if axis == position else 1 for axis in range(len(shape))])
    return gain


def scatter_about(own_key, dims, scale, reach, pieces=(), held_as=jnp.bfloat16):
    entries = scale * jax.random.normal(own_key, dims, jnp.float32)
    if pieces:
        entries = entries * block_scale(own_key, dims, pieces, -0.22, 0.18)
    return jnp.clip(entries, -reach, reach).astype(held_as)


def setup_inputs(seed: int = 0) -> dict:
    splits = jax.random.split(jax.random.key(seed), 10)
    return {
        "grad_parts": draw_grad_parts(jax.random.fold_in(splits[9], 71), 0),
        "master": scatter_about(splits[1], (D, 2 * KVH * HD), D ** -0.5, 0.078125, ((0, 128), (1, 8)), jnp.float32),
        "moment_one": scatter_about(splits[2], (D, 2 * KVH * HD), 0.1, 1.5, ((0, 128), (1, 8)), jnp.float32),
        "moment_two": jnp.clip(jnp.exp(math.log(0.03) - 2.3025851 * jax.random.uniform(splits[3], (D, 2 * KVH * HD), jnp.float32) ** block_scale(splits[3], (D, 2 * KVH * HD), ((0, 128), (1, 8)), -0.2, 0.2)), 0.003, 0.03),
        "hidden_in": scatter_about(splits[4], (ROWS, STEPS, D), 1.0, 6.0, ((0, 128),)),
        "queries": draw_queries(jax.random.fold_in(splits[9], 71), 0),
        "cache_keys": draw_cache_keys(jax.random.fold_in(splits[9], 71), 0),
        "cache_values": scatter_about(splits[7], (ROWS, CACHE, KVH * HD), 1.0, 6.0, ((0, 128), (2, 8))),
        "cache_lengths": plant(jax.random.randint(splits[8], (ROWS,), 16, CACHE + 1), jax.random.fold_in(splits[8], 1), 16, CACHE).astype(jnp.int32),
    }


BETA_ONE = 0.9
BETA_TWO = 0.999
FIRST_CORR = 0.9999734386011124
SECOND_CORR = 0.09520785288629041
LEARN_RATE = 0.003
EPSILON = 1e-08
ROPE_BASE = 1000000.0
NEG_FILL = -1e+30

def rotate(new_keys, lengths):
    positions = (lengths[:, None] + jnp.arange(new_keys.shape[1], dtype=jnp.int32)[None, :]).astype(jnp.float32)
    half_dim = new_keys.shape[-1] // 2
    inverse = jnp.exp(-math.log(ROPE_BASE) * 2.0 * jnp.arange(half_dim, dtype=jnp.float32) / new_keys.shape[-1])
    angles = positions[:, :, None] * inverse[None, None, :]
    cosine_part = jnp.concatenate([jnp.cos(angles), jnp.cos(angles)], -1)[:, :, None, :]
    sine_part = jnp.concatenate([jnp.sin(angles), jnp.sin(angles)], -1)[:, :, None, :]
    rotated = jnp.concatenate([-new_keys[..., half_dim:], new_keys[..., :half_dim]], -1)
    return new_keys * cosine_part + rotated * sine_part

def attend_row(items):
    query_row, old_keys, old_values, length, new_keys, new_values = items
    groups = QH // KVH
    query_heads = query_row.reshape(STEPS, KVH, groups, HD).astype(jnp.float32)
    old_k = old_keys.reshape(CACHE, KVH, HD).astype(jnp.float32)
    old_v = old_values.reshape(CACHE, KVH, HD).astype(jnp.float32)
    scaling = 1.0 / math.sqrt(HD)
    old_scores = jnp.einsum('sagd,jad->sagj', query_heads, old_k) * scaling
    valid_slots = jnp.arange(CACHE, dtype=jnp.int32) < length
    old_scores = jnp.where(valid_slots[None, None, None, :], old_scores, NEG_FILL)
    new_scores = jnp.einsum('sagd,tad->sagt', query_heads, new_keys.astype(jnp.float32)) * scaling
    causal = jnp.arange(STEPS)[:, None] >= jnp.arange(STEPS)[None, :]
    new_scores = jnp.where(causal[:, None, None, :], new_scores, NEG_FILL)
    scores = jnp.concatenate([old_scores, new_scores], -1)
    row_max = lax.optimization_barrier(jnp.max(scores, -1, keepdims=True))
    exp_scores = jnp.exp(scores - row_max)
    probs = (exp_scores / lax.optimization_barrier(jnp.sum(exp_scores, -1, keepdims=True))).astype(jnp.bfloat16)
    output = jnp.einsum('sagj,jad->sagd', probs[..., :CACHE].astype(jnp.float32), old_v)
    output = output + jnp.einsum('sagt,tad->sagd', probs[..., CACHE:].astype(jnp.float32), new_values.astype(jnp.float32))
    return output.reshape(STEPS, QH * HD).astype(jnp.bfloat16)

def reference(grad_parts, master, moment_one, moment_two, hidden_in, queries, cache_keys, cache_values, cache_lengths):
    grad_sum = lax.optimization_barrier(jnp.sum(grad_parts, axis=0))
    squares = jnp.sum(grad_sum * grad_sum)
    norm_limit = math.sqrt(D * 2 * KVH * HD)
    clipped = grad_sum * jnp.minimum(1.0, norm_limit / jnp.sqrt(squares))
    new_moment_one = BETA_ONE * moment_one + (1.0 - BETA_ONE) * clipped
    new_moment_two = BETA_TWO * moment_two + (1.0 - BETA_TWO) * clipped * clipped
    update = new_moment_one / FIRST_CORR / (jnp.sqrt(new_moment_two / SECOND_CORR) + EPSILON)
    weights = (master - LEARN_RATE * update).astype(jnp.bfloat16)
    projected = jnp.dot(hidden_in.reshape(ROWS * STEPS, D), weights, preferred_element_type=jnp.float32)
    projected = projected.reshape(ROWS, STEPS, KVH, 2, HD)
    new_keys = rotate(projected[:, :, :, 0, :], cache_lengths).astype(jnp.bfloat16)
    new_values = projected[:, :, :, 1, :].astype(jnp.bfloat16)
    new_entries = jnp.stack([new_keys, new_values], 3).reshape(ROWS, STEPS, 2 * KVH * HD)
    attended = lax.map(attend_row, (queries, cache_keys, cache_values, cache_lengths, new_keys, new_values))
    return (new_moment_one, new_moment_two, new_entries, attended)
```

```python
import math

import jax
import jax.numpy as jnp
from jax import lax
from jax.experimental import pallas as pl
from jax.experimental.pallas import tpu as pltpu
from jax.sharding import Mesh
from jax.sharding import PartitionSpec as P

D = 5120
QH = 40
KVH = 8
HD = 128
GROUPS = QH // KVH
ZH, ZL = 8, 4
TP = ("y", "c")
REP = ("zh", "zl", "xl")
GRP_REP = ("g",) + REP
SPLIT = ("g", "zl", "xl")
PLANE = ("g", "xl", "y", "c")
LINE = ("zh", "zl")
QROWS = 24

BETA_ONE = 0.9
BETA_TWO = 0.999
FIRST_CORR = 0.9999734386011124
SECOND_CORR = 0.09520785288629041
LEARN_RATE = 0.003
EPSILON = 1e-08
ROPE_BASE = 1000000.0
NEG_FILL = -1e30


def copies_from(array, axes):
    size = math.prod(lax.axis_size(a) for a in axes)
    copies = jnp.broadcast_to(array[None], (size, *array.shape))
    return lax.all_to_all(copies, axes, split_axis=0, concat_axis=0, tiled=True)


def regroup_kernel(x_ref, out_ref):
    x = x_ref[...].astype(jnp.float32)
    step = D // (2 * ZH * ZL * 2)
    for g in range(2):
        for j in range(ZL * 2):
            cols = []
            for zh in range(ZH):
                start = ((g * ZH + zh) * ZL * 2 + j) * step
                cols.append(x[:, start : start + step])
            out_ref[g * ZL * 2 + j] = jnp.concatenate(cols, axis=1).astype(jnp.bfloat16)


def cache_kernel(len_ref, q_ref, k_ref, v_ref, qs_ref, acc_ref, max_ref, sum_ref, qf_ref):
    rows, slots = k_ref.shape[0], k_ref.shape[1]
    steps = q_ref.shape[1]
    qf_ref[...] = jnp.zeros_like(qf_ref)
    for r in range(rows):
        q = q_ref[r].astype(jnp.float32)
        for h in range(GROUPS):
            qf_ref[pl.ds(r * QROWS + h * steps, steps), :] = q[:, h * HD : (h + 1) * HD]
    qs_ref[...] = qf_ref[...].astype(jnp.bfloat16)
    slot = lax.broadcasted_iota(jnp.int32, (QROWS, slots), 1)
    for r in range(rows):
        qb = qf_ref[pl.ds(r * QROWS, QROWS), :].astype(jnp.bfloat16)
        s = lax.dot_general(qb, k_ref[r], (((1,), (1,)), ((), ())), preferred_element_type=jnp.float32)
        s = jnp.where(slot < len_ref[r], s * (1.0 / math.sqrt(HD)), NEG_FILL)
        top = jnp.max(s, axis=1, keepdims=True)
        p = jnp.exp(s - top)
        total = jnp.sum(p, axis=1, keepdims=True)
        acc = jnp.dot(p.astype(jnp.bfloat16), v_ref[r], preferred_element_type=jnp.float32)
        at = pl.ds(r * QROWS, QROWS)
        acc_ref[at, :] = acc
        max_ref[at, :] = jnp.broadcast_to(top, (QROWS, HD))
        sum_ref[at, :] = jnp.broadcast_to(total, (QROWS, HD))


def tail_kernel(part_ref, cos_ref, sin_ref, q_ref, acc_ref, max_ref, sum_ref, new_ref, out_ref, o_ref):
    tokens = part_ref.shape[1]
    rows, steps = out_ref.shape[0], out_ref.shape[1]
    projected = part_ref[0].astype(jnp.float32)
    for i in range(1, part_ref.shape[0]):
        projected = projected + part_ref[i].astype(jnp.float32)
    k, v = projected[:, :HD], projected[:, HD:]
    turned = pltpu.roll(k, HD // 2, 1)
    k = k * cos_ref[...] + turned * sin_ref[...]
    kb, vb = k.astype(jnp.bfloat16), v.astype(jnp.bfloat16)
    new_ref[:, :HD] = kb
    new_ref[:, HD:] = vb
    total_q = q_ref.shape[0]
    s = lax.dot_general(q_ref[...], kb, (((1,), (1,)), ((), ())), preferred_element_type=jnp.float32)
    s = s * (1.0 / math.sqrt(HD))
    q_at = lax.broadcasted_iota(jnp.int32, (total_q, tokens), 0)
    t_at = lax.broadcasted_iota(jnp.int32, (total_q, tokens), 1)
    ok = t_at < 0
    for r in range(rows):
        inside = (q_at >= r * QROWS) & (q_at < (r + 1) * QROWS) & (t_at >= r * steps)
        ok = ok | (inside & (t_at <= r * steps + (q_at & (steps - 1))))
    s = jnp.where(ok, s, NEG_FILL)
    top = jnp.maximum(jnp.max(s, axis=1, keepdims=True), max_ref[...])
    p = jnp.where(ok, jnp.exp(s - top[:, :1]), 0.0)
    fade = jnp.exp(max_ref[...] - top)
    total = sum_ref[...] * fade + jnp.sum(p, axis=1, keepdims=True)
    acc = acc_ref[...] * fade + jnp.dot(p.astype(jnp.bfloat16), vb, preferred_element_type=jnp.float32)
    o_ref[...] = acc / total
    for r in range(rows):
        for h in range(GROUPS):
            out_ref[r, :, h * HD : (h + 1) * HD] = o_ref[pl.ds(r * QROWS + h * steps, steps), :].astype(jnp.bfloat16)


VMEM = pl.BlockSpec(memory_space=pltpu.VMEM)
SMEM = pl.BlockSpec(memory_space=pltpu.SMEM)


def body(grad_parts, master, moment_one, moment_two, hidden_in, queries, cache_keys, cache_values, cache_lengths):
    k_rows, col_width = master.shape
    row_count, step_count, model_width = hidden_in.shape
    tokens = row_count * step_count
    n_split = 2 * ZL * 2
    all_q = row_count * QROWS

    flat = hidden_in.reshape(tokens, model_width)
    blocks = pl.pallas_call(
        regroup_kernel,
        out_shape=jax.ShapeDtypeStruct((n_split, tokens, model_width // n_split), jnp.bfloat16),
        in_specs=[VMEM],
        out_specs=VMEM,
    )(flat)
    inputs = lax.all_to_all(blocks, SPLIT, split_axis=0, concat_axis=0, tiled=True)
    inputs = inputs.reshape(n_split * tokens, model_width // n_split)

    q_rows, old_acc, old_max, old_sum = pl.pallas_call(
        cache_kernel,
        out_shape=(
            jax.ShapeDtypeStruct((all_q, HD), jnp.bfloat16),
            jax.ShapeDtypeStruct((all_q, HD), jnp.float32),
            jax.ShapeDtypeStruct((all_q, HD), jnp.float32),
            jax.ShapeDtypeStruct((all_q, HD), jnp.float32),
        ),
        in_specs=[SMEM, VMEM, VMEM, VMEM],
        out_specs=(VMEM,) * 4,
        scratch_shapes=[pltpu.VMEM((all_q, HD), jnp.float32)],
    )(cache_lengths, queries, cache_keys, cache_values)

    half = HD // 2
    inverse = jnp.exp(-math.log(ROPE_BASE) * 2.0 * jnp.arange(half, dtype=jnp.float32) / HD)
    positions = (cache_lengths[:, None] + jnp.arange(step_count, dtype=jnp.int32)[None, :]).astype(jnp.float32)
    angles = positions.reshape(tokens, 1) * inverse[None, :]
    cosine, sine = jnp.cos(angles), jnp.sin(angles)
    cosine = jnp.concatenate([cosine, cosine], -1)
    sine = jnp.concatenate([-sine, sine], -1)

    tiles = jnp.moveaxis(grad_parts[0].reshape(k_rows, 8, col_width), 1, 0)
    grad_sum = lax.all_to_all(tiles, TP, split_axis=0, concat_axis=0, tiled=True).sum(axis=0)
    squares = jnp.full((1, HD), jnp.sum(grad_sum * grad_sum), jnp.float32)
    squares = copies_from(squares, PLANE).sum(axis=0)
    squares = copies_from(squares, LINE).sum(axis=0)[0, 0]
    norm_limit = math.sqrt(D * 2 * KVH * HD)
    clipped = grad_sum * jnp.minimum(1.0, norm_limit / jnp.sqrt(squares))
    new_moment_one = BETA_ONE * moment_one + (1.0 - BETA_ONE) * clipped
    new_moment_two = BETA_TWO * moment_two + (1.0 - BETA_TWO) * clipped * clipped
    update = new_moment_one / FIRST_CORR / (jnp.sqrt(new_moment_two / SECOND_CORR) + EPSILON)
    weights = (master - LEARN_RATE * update).astype(jnp.bfloat16)

    rows_here = copies_from(weights, ("zh",)).reshape(ZH * k_rows, col_width)
    shares = jnp.dot(inputs, rows_here, preferred_element_type=jnp.float32)
    shares = shares.reshape(n_split, tokens, col_width)
    parts = lax.all_to_all(shares, SPLIT, split_axis=0, concat_axis=0, tiled=True)

    entries, attended = pl.pallas_call(
        tail_kernel,
        out_shape=(
            jax.ShapeDtypeStruct((tokens, col_width), jnp.bfloat16),
            jax.ShapeDtypeStruct((row_count, step_count, GROUPS * HD), jnp.bfloat16),
        ),
        in_specs=[VMEM] * 7,
        out_specs=(VMEM,) * 2,
        scratch_shapes=[pltpu.VMEM((all_q, HD), jnp.float32)],
    )(parts, cosine, sine, q_rows, old_acc, old_max, old_sum)
    return (new_moment_one, new_moment_two, entries.reshape(row_count, step_count, col_width), attended)


def solution(mesh):
    torus = Mesh(mesh.devices.reshape(2, ZH, ZL, 2, 4, 2), ("g", "zh", "zl", "xl", "y", "c"))
    return jax.shard_map(
        body,
        mesh=torus,
        in_specs=(
            P(TP, GRP_REP, None),
            P(GRP_REP, TP),
            P(GRP_REP, TP),
            P(GRP_REP, TP),
            P(GRP_REP, None, None),
            P(GRP_REP, None, TP),
            P(GRP_REP, None, TP),
            P(GRP_REP, None, TP),
            P(GRP_REP),
        ),
        out_specs=(P(GRP_REP, TP), P(GRP_REP, TP), P(GRP_REP, None, TP), P(GRP_REP, None, TP)),
        check_vma=False,
    )
```

```python
import math

import jax
import jax.numpy as jnp
import numpy as np
from jax import lax
from jax.experimental import pallas as pl
from jax.experimental.pallas import tpu as pltpu
from jax.sharding import Mesh
from jax.sharding import PartitionSpec as P

D = 5120
QH = 40
KVH = 8
HD = 128
GROUPS = QH // KVH
ZH, ZL = 8, 4
TP = ("y", "c")
REP = ("zh", "zl", "xl")
GRP_REP = ("g",) + REP
SPLIT = ("zl", "g", "xl")
PLANE = ("g", "xl", "y", "c")
LINE = ("zh", "zl")
QROWS = 24

BETA_ONE = 0.9
BETA_TWO = 0.999
FIRST_CORR = 0.9999734386011124
SECOND_CORR = 0.09520785288629041
LEARN_RATE = 0.003
EPSILON = 1e-08
ROPE_BASE = 1000000.0
NEG_FILL = -1e30


def copies_from(array, axes):
    size = math.prod(lax.axis_size(a) for a in axes)
    copies = jnp.broadcast_to(array[None], (size, *array.shape))
    return lax.all_to_all(copies, axes, split_axis=0, concat_axis=0, tiled=True)


def near(array):
    return pltpu.with_memory_space_constraint(array, pltpu.VMEM)


def moved(blocks, axes):
    size = len(blocks)
    out = [blocks[0]]
    for k in range(1, size):
        out.append(near(lax.ppermute(blocks[k], axes, [(i, (i + k) % size) for i in range(size)])))
    return out


def regroup_kernel(at_ref, x_ref, *refs):
    outs, flat_ref, all_ref = refs[:4], refs[4], refs[5]
    rows, steps, width = x_ref.shape
    for r in range(rows):
        flat_ref[pl.ds(r * steps, steps), :] = x_ref[r].astype(jnp.float32)
    step = width // (ZH * ZL * 4)
    for x in range(4):
        for zl in range(ZL):
            cols = []
            for zh in range(ZH):
                start = (((x // 2 * ZH + zh) * ZL + zl) * 2 + x % 2) * step
                cols.append(flat_ref[:, start : start + step])
            all_ref[x, zl] = jnp.concatenate(cols, axis=1).astype(jnp.bfloat16)
    for k in range(4):
        outs[k][...] = all_ref[(at_ref[0] + k) & 3]


def turn_kernel(at_ref, *refs):
    for k in range(4):
        for j in range(4):
            refs[4 + k][(at_ref[0] - j) & 3] = refs[j][(at_ref[1] + k) & 3]


def product_kernel(at_ref, w_ref, *refs):
    out_ref = refs[4]
    n, tokens, depth = refs[0].shape
    for k in range(4):
        part = jnp.dot(refs[k][...].reshape(n * tokens, depth), w_ref[...], preferred_element_type=jnp.float32)
        out_ref[(at_ref[1] - k) & 3] = part.reshape(n, tokens, -1)


def cache_kernel(len_ref, q_ref, k_ref, v_ref, qs_ref, acc_ref, max_ref, sum_ref, qf_ref):
    rows, slots = k_ref.shape[0], k_ref.shape[1]
    steps = q_ref.shape[1]
    qf_ref[...] = jnp.zeros_like(qf_ref)
    for r in range(rows):
        q = q_ref[r].astype(jnp.float32)
        for h in range(GROUPS):
            qf_ref[pl.ds(r * QROWS + h * steps, steps), :] = q[:, h * HD : (h + 1) * HD]
    qs_ref[...] = qf_ref[...].astype(jnp.bfloat16)
    slot = lax.broadcasted_iota(jnp.int32, (QROWS, slots), 1)
    for r in range(rows):
        qb = qf_ref[pl.ds(r * QROWS, QROWS), :].astype(jnp.bfloat16)
        s = lax.dot_general(qb, k_ref[r], (((1,), (1,)), ((), ())), preferred_element_type=jnp.float32)
        s = jnp.where(slot < len_ref[r], s * (1.0 / math.sqrt(HD)), NEG_FILL)
        top = jnp.max(s, axis=1, keepdims=True)
        p = jnp.exp(s - top)
        total = jnp.sum(p, axis=1, keepdims=True)
        acc = jnp.dot(p.astype(jnp.bfloat16), v_ref[r], preferred_element_type=jnp.float32)
        at = pl.ds(r * QROWS, QROWS)
        acc_ref[at, :] = acc
        max_ref[at, :] = jnp.broadcast_to(top, (QROWS, HD))
        sum_ref[at, :] = jnp.broadcast_to(total, (QROWS, HD))


def tail_kernel(part_ref, cos_ref, sin_ref, q_ref, acc_ref, max_ref, sum_ref, new_ref, out_ref, o_ref, n_ref):
    tokens = part_ref.shape[1]
    rows, steps = out_ref.shape[0], out_ref.shape[1]
    projected = part_ref[0].astype(jnp.float32)
    for i in range(1, part_ref.shape[0]):
        projected = projected + part_ref[i].astype(jnp.float32)
    k, v = projected[:, :HD], projected[:, HD:]
    turned = pltpu.roll(k, HD // 2, 1)
    k = k * cos_ref[...] + turned * sin_ref[...]
    kb, vb = k.astype(jnp.bfloat16), v.astype(jnp.bfloat16)
    n_ref[:, :HD] = k
    n_ref[:, HD:] = v
    for r in range(rows):
        new_ref[r] = n_ref[pl.ds(r * steps, steps), :].astype(jnp.bfloat16)
    total_q = q_ref.shape[0]
    s = lax.dot_general(q_ref[...], kb, (((1,), (1,)), ((), ())), preferred_element_type=jnp.float32)
    s = s * (1.0 / math.sqrt(HD))
    q_at = lax.broadcasted_iota(jnp.int32, (total_q, tokens), 0)
    t_at = lax.broadcasted_iota(jnp.int32, (total_q, tokens), 1)
    ok = t_at < 0
    for r in range(rows):
        inside = (q_at >= r * QROWS) & (q_at < (r + 1) * QROWS) & (t_at >= r * steps)
        ok = ok | (inside & (t_at <= r * steps + (q_at & (steps - 1))))
    s = jnp.where(ok, s, NEG_FILL)
    top = jnp.maximum(jnp.max(s, axis=1, keepdims=True), max_ref[...])
    p = jnp.where(ok, jnp.exp(s - top[:, :1]), 0.0)
    fade = jnp.exp(max_ref[...] - top)
    total = sum_ref[...] * fade + jnp.sum(p, axis=1, keepdims=True)
    acc = acc_ref[...] * fade + jnp.dot(p.astype(jnp.bfloat16), vb, preferred_element_type=jnp.float32)
    o_ref[...] = acc / total
    for r in range(rows):
        for h in range(GROUPS):
            out_ref[r, :, h * HD : (h + 1) * HD] = o_ref[pl.ds(r * QROWS + h * steps, steps), :].astype(jnp.bfloat16)


VMEM = pl.BlockSpec(memory_space=pltpu.VMEM)
SMEM = pl.BlockSpec(memory_space=pltpu.SMEM)


def body(grad_parts, master, moment_one, moment_two, hidden_in, queries, cache_keys, cache_values, cache_lengths):
    k_rows, col_width = master.shape
    row_count, step_count, model_width = hidden_in.shape
    tokens = row_count * step_count
    n_split = 2 * ZL * 2
    all_q = row_count * QROWS

    tiles = jnp.moveaxis(grad_parts[0].reshape(k_rows, 8, col_width), 1, 0)
    grad_sum = lax.all_to_all(tiles, TP, split_axis=0, concat_axis=0, tiled=True).sum(axis=0)
    squares = jnp.sum(grad_sum * grad_sum, axis=0).reshape(2, HD)
    squares = copies_from(squares, PLANE).sum(axis=0)

    squares, hidden_in, cache_lengths = lax.optimization_barrier((squares, hidden_in, cache_lengths))
    block = jax.ShapeDtypeStruct((4, tokens, model_width // n_split), jnp.bfloat16)
    at = jnp.stack([lax.axis_index("g") * 2 + lax.axis_index("xl"), lax.axis_index("zl")]).astype(jnp.int32)
    along_x = pl.pallas_call(
        regroup_kernel,
        out_shape=(block,) * 4,
        in_specs=[SMEM, VMEM],
        out_specs=(VMEM,) * 4,
        scratch_shapes=[
            pltpu.VMEM((tokens, model_width), jnp.float32),
            pltpu.VMEM((4, ZL, tokens, model_width // n_split), jnp.bfloat16),
        ],
    )(at, hidden_in)
    along_x = moved(along_x, ("g", "xl"))

    q_rows, old_acc, old_max, old_sum = pl.pallas_call(
        cache_kernel,
        out_shape=(
            jax.ShapeDtypeStruct((all_q, HD), jnp.bfloat16),
            jax.ShapeDtypeStruct((all_q, HD), jnp.float32),
            jax.ShapeDtypeStruct((all_q, HD), jnp.float32),
            jax.ShapeDtypeStruct((all_q, HD), jnp.float32),
        ),
        in_specs=[SMEM, VMEM, VMEM, VMEM],
        out_specs=(VMEM,) * 4,
        scratch_shapes=[pltpu.VMEM((all_q, HD), jnp.float32)],
    )(cache_lengths, queries, cache_keys, cache_values)

    half = HD // 2
    inverse = jnp.asarray(ROPE_BASE ** (-2.0 * np.arange(half) / HD), jnp.float32)
    positions = (cache_lengths[:, None] + jnp.arange(step_count, dtype=jnp.int32)[None, :]).astype(jnp.float32)
    turns = positions.reshape(tokens, 1) * inverse[None, :]
    cosine, sine = jnp.cos(turns), jnp.sin(turns)
    cosine = jnp.concatenate([cosine, cosine], -1)
    sine = jnp.concatenate([-sine, sine], -1)

    cached, angles = (q_rows, old_acc, old_max, old_sum), (cosine, sine)
    squares, along_x, cached, angles = lax.optimization_barrier((copies_from(squares, LINE), along_x, cached, angles))
    squares = jnp.sum(squares)
    along_z = pl.pallas_call(turn_kernel, out_shape=(block,) * 4, in_specs=[SMEM] + [VMEM] * 4, out_specs=(VMEM,) * 4)(
        at, *along_x
    )
    inputs = moved(along_z, ("zl",))
    norm_limit = math.sqrt(D * 2 * KVH * HD)
    clipped = grad_sum * jnp.minimum(1.0, norm_limit / jnp.sqrt(squares))
    new_moment_one = BETA_ONE * moment_one + (1.0 - BETA_ONE) * clipped
    new_moment_two = BETA_TWO * moment_two + (1.0 - BETA_TWO) * clipped * clipped
    update = new_moment_one / FIRST_CORR / (jnp.sqrt(new_moment_two / SECOND_CORR) + EPSILON)
    weights = (master - LEARN_RATE * update).astype(jnp.bfloat16)

    rows_here = near(copies_from(weights, ("zh",)).reshape(ZH * k_rows, col_width))
    shares = pl.pallas_call(
        product_kernel,
        out_shape=jax.ShapeDtypeStruct((ZL, 4, tokens, col_width), jnp.float32),
        in_specs=[SMEM] + [VMEM] * 5,
        out_specs=VMEM,
    )(at, rows_here, *inputs)
    shares = shares.reshape(n_split, tokens, col_width)
    parts = lax.all_to_all(shares, SPLIT, split_axis=0, concat_axis=0, tiled=True)

    entries, attended = pl.pallas_call(
        tail_kernel,
        out_shape=(
            jax.ShapeDtypeStruct((row_count, step_count, col_width), jnp.bfloat16),
            jax.ShapeDtypeStruct((row_count, step_count, GROUPS * HD), jnp.bfloat16),
        ),
        in_specs=[VMEM] * 7,
        out_specs=(VMEM,) * 2,
        scratch_shapes=[pltpu.VMEM((all_q, HD), jnp.float32), pltpu.VMEM((tokens, col_width), jnp.float32)],
    )(near(parts), *angles, *cached)
    return (new_moment_one, new_moment_two, entries, attended)


def solution(mesh):
    torus = Mesh(mesh.devices.reshape(2, ZH, ZL, 2, 4, 2), ("g", "zh", "zl", "xl", "y", "c"))
    return jax.shard_map(
        body,
        mesh=torus,
        in_specs=(
            P(TP, GRP_REP, None),
            P(GRP_REP, TP),
            P(GRP_REP, TP),
            P(GRP_REP, TP),
            P(GRP_REP, None, None),
            P(GRP_REP, None, TP),
            P(GRP_REP, None, TP),
            P(GRP_REP, None, TP),
            P(GRP_REP),
        ),
        out_specs=(P(GRP_REP, TP), P(GRP_REP, TP), P(GRP_REP, None, TP), P(GRP_REP, None, TP)),
        check_vma=False,
    )
```

```python
import functools
import math

import jax
import jax.numpy as jnp
import numpy as np
from jax import lax
from jax.experimental import pallas as pl
from jax.experimental.pallas import tpu as pltpu
from jax.sharding import Mesh
from jax.sharding import PartitionSpec as P

D = 5120
QH = 40
KVH = 8
HD = 128
GROUPS = QH // KVH
ZH, ZL = 8, 4
TP = ("y", "c")
REP = ("zh", "zl", "xl")
GRP_REP = ("g",) + REP
SPLIT = ("zl", "g", "xl")
ORDER = tuple((i + 5) % ZH for i in range(ZH))
QROWS = 24

BETA_ONE = 0.9
BETA_TWO = 0.999
FIRST_CORR = 0.9999734386011124
SECOND_CORR = 0.09520785288629041
LEARN_RATE = 0.003
EPSILON = 1e-08
ROPE_BASE = 1000000.0
NEG_FILL = -1e30


def swapped(blocks, axes, groups=None):
    return lax.all_to_all(blocks, axes, split_axis=0, concat_axis=0, tiled=True, axis_index_groups=groups)


def near(array):
    return pltpu.with_memory_space_constraint(array, pltpu.VMEM)


def regroup_kernel(x_ref, out_ref, flat_ref):
    rows, steps, width = x_ref.shape
    for r in range(rows):
        flat_ref[pl.ds(r * steps, steps), :] = x_ref[r].astype(jnp.float32)
    step = width // (ZH * ZL * 4)
    room = jnp.zeros((rows * steps, out_ref.shape[2] - ZH * step), jnp.float32)
    for zl in range(ZL):
        for x in range(4):
            cols = []
            for zh in ORDER:
                start = (((x // 2 * ZH + zh) * ZL + zl) * 2 + x % 2) * step
                cols.append(flat_ref[:, start : start + step])
            out_ref[zl * 4 + x] = jnp.concatenate(cols + [room], axis=1).astype(jnp.bfloat16)


def norm_kernel(parts_ref, blocks_ref, sum_ref, out_ref, *, width):
    total = parts_ref[0]
    for i in range(1, parts_ref.shape[0]):
        total = total + parts_ref[i]
    sum_ref[...] = total
    squares = jnp.sum(jnp.sum(total * total, axis=0, keepdims=True), axis=1, keepdims=True)
    high = squares.astype(jnp.bfloat16).astype(jnp.float32)
    rest = squares - high
    middle = rest.astype(jnp.bfloat16).astype(jnp.float32)
    low = rest - middle
    row = lax.broadcasted_iota(jnp.int32, blocks_ref.shape[1:], 0)
    lane = lax.broadcasted_iota(jnp.int32, blocks_ref.shape[1:], 1)
    terms = jnp.where(row == 0, high, jnp.where(row == 1, middle, jnp.where(row == 2, low, 0.0)))
    terms = jnp.where(lane >= width, terms, 0.0).astype(jnp.bfloat16)
    for i in range(blocks_ref.shape[0]):
        out_ref[i] = blocks_ref[i] + terms


def update_kernel(squares_ref, sum_ref, master_ref, one_ref, two_ref, new_one_ref, new_two_ref, copies_ref):
    squares = jnp.sum(squares_ref[...], axis=0)
    scale = jnp.minimum(1.0, math.sqrt(D * 2 * KVH * HD) / jnp.sqrt(squares))[:, :1]
    clipped = sum_ref[...] * scale
    one = BETA_ONE * one_ref[...] + (1.0 - BETA_ONE) * clipped
    two = BETA_TWO * two_ref[...] + (1.0 - BETA_TWO) * clipped * clipped
    new_one_ref[...] = one
    new_two_ref[...] = two
    update = one / FIRST_CORR / (jnp.sqrt(two / SECOND_CORR) + EPSILON)
    weights = (master_ref[...] - LEARN_RATE * update).astype(jnp.bfloat16)
    for i in range(copies_ref.shape[0]):
        copies_ref[i] = weights


def cache_kernel(len_ref, q_ref, k_ref, v_ref, qs_ref, acc_ref, max_ref, sum_ref, qf_ref):
    rows, slots = k_ref.shape[0], k_ref.shape[1]
    steps = q_ref.shape[1]
    qf_ref[...] = jnp.zeros_like(qf_ref)
    for r in range(rows):
        q = q_ref[r].astype(jnp.float32)
        for h in range(GROUPS):
            qf_ref[pl.ds(r * QROWS + h * steps, steps), :] = q[:, h * HD : (h + 1) * HD]
    qs_ref[...] = qf_ref[...].astype(jnp.bfloat16)
    slot = lax.broadcasted_iota(jnp.int32, (QROWS, slots), 1)
    for r in range(rows):
        qb = qf_ref[pl.ds(r * QROWS, QROWS), :].astype(jnp.bfloat16)
        s = lax.dot_general(qb, k_ref[r], (((1,), (1,)), ((), ())), preferred_element_type=jnp.float32)
        s = jnp.where(slot < len_ref[r], s * (1.0 / math.sqrt(HD)), NEG_FILL)
        top = jnp.max(s, axis=1, keepdims=True)
        p = jnp.exp(s - top)
        total = jnp.sum(p, axis=1, keepdims=True)
        acc = jnp.dot(p.astype(jnp.bfloat16), v_ref[r], preferred_element_type=jnp.float32)
        at = pl.ds(r * QROWS, QROWS)
        acc_ref[at, :] = acc
        max_ref[at, :] = jnp.broadcast_to(top, (QROWS, HD))
        sum_ref[at, :] = jnp.broadcast_to(total, (QROWS, HD))


def tail_kernel(part_ref, cos_ref, sin_ref, q_ref, acc_ref, max_ref, sum_ref, new_ref, out_ref, o_ref, n_ref):
    tokens = part_ref.shape[1]
    rows, steps = out_ref.shape[0], out_ref.shape[1]
    projected = part_ref[0].astype(jnp.float32)
    for i in range(1, part_ref.shape[0]):
        projected = projected + part_ref[i].astype(jnp.float32)
    k, v = projected[:, :HD], projected[:, HD:]
    turned = pltpu.roll(k, HD // 2, 1)
    k = k * cos_ref[...] + turned * sin_ref[...]
    kb, vb = k.astype(jnp.bfloat16), v.astype(jnp.bfloat16)
    n_ref[:, :HD] = k
    n_ref[:, HD:] = v
    for r in range(rows):
        new_ref[r] = n_ref[pl.ds(r * steps, steps), :].astype(jnp.bfloat16)
    total_q = q_ref.shape[0]
    s = lax.dot_general(q_ref[...], kb, (((1,), (1,)), ((), ())), preferred_element_type=jnp.float32)
    s = s * (1.0 / math.sqrt(HD))
    q_at = lax.broadcasted_iota(jnp.int32, (total_q, tokens), 0)
    t_at = lax.broadcasted_iota(jnp.int32, (total_q, tokens), 1)
    ok = t_at < 0
    for r in range(rows):
        inside = (q_at >= r * QROWS) & (q_at < (r + 1) * QROWS) & (t_at >= r * steps)
        ok = ok | (inside & (t_at <= r * steps + (q_at & (steps - 1))))
    s = jnp.where(ok, s, NEG_FILL)
    top = jnp.maximum(jnp.max(s, axis=1, keepdims=True), max_ref[...])
    p = jnp.where(ok, jnp.exp(s - top[:, :1]), 0.0)
    fade = jnp.exp(max_ref[...] - top)
    total = sum_ref[...] * fade + jnp.sum(p, axis=1, keepdims=True)
    acc = acc_ref[...] * fade + jnp.dot(p.astype(jnp.bfloat16), vb, preferred_element_type=jnp.float32)
    o_ref[...] = acc / total
    for r in range(rows):
        for h in range(GROUPS):
            out_ref[r, :, h * HD : (h + 1) * HD] = o_ref[pl.ds(r * QROWS + h * steps, steps), :].astype(jnp.bfloat16)


VMEM = pl.BlockSpec(memory_space=pltpu.VMEM)
SMEM = pl.BlockSpec(memory_space=pltpu.SMEM)


def body(grad_parts, master, moment_one, moment_two, hidden_in, queries, cache_keys, cache_values, cache_lengths):
    k_rows, col_width = master.shape
    row_count, step_count, model_width = hidden_in.shape
    tokens = row_count * step_count
    n_split = 4 * ZL
    n_tp = 8
    depth = model_width // n_split
    all_q = row_count * QROWS

    blocks = pl.pallas_call(
        regroup_kernel,
        out_shape=jax.ShapeDtypeStruct((n_split, tokens, depth + 64), jnp.bfloat16),
        in_specs=[VMEM],
        out_specs=VMEM,
        scratch_shapes=[pltpu.VMEM((tokens, model_width), jnp.float32)],
    )(hidden_in)

    tiles = jnp.moveaxis(grad_parts[0].reshape(k_rows, n_tp, col_width), 1, 0)
    arrived = swapped(tiles, TP)
    grad_sum, blocks = pl.pallas_call(
        functools.partial(norm_kernel, width=depth),
        out_shape=(
            jax.ShapeDtypeStruct((k_rows, col_width), jnp.float32),
            jax.ShapeDtypeStruct(blocks.shape, jnp.bfloat16),
        ),
        in_specs=[VMEM] * 2,
        out_specs=(VMEM,) * 2,
    )(near(arrived), near(blocks))
    blocks = swapped(blocks, SPLIT)
    squares = jnp.sum(blocks[:, :3, depth].astype(jnp.float32))
    blocks, squares, cache_lengths = lax.optimization_barrier((blocks, squares, cache_lengths))
    inputs = blocks[:, :, :depth].reshape(n_split * tokens, depth)
    peers = [zh * n_tp + t for zh in ORDER for t in range(n_tp)]
    squares = swapped(jnp.full((ZH * n_tp, 1, HD), squares), ("zh",) + TP, [peers])

    q_rows, old_acc, old_max, old_sum = pl.pallas_call(
        cache_kernel,
        out_shape=(
            jax.ShapeDtypeStruct((all_q, HD), jnp.bfloat16),
            jax.ShapeDtypeStruct((all_q, HD), jnp.float32),
            jax.ShapeDtypeStruct((all_q, HD), jnp.float32),
            jax.ShapeDtypeStruct((all_q, HD), jnp.float32),
        ),
        in_specs=[SMEM, VMEM, VMEM, VMEM],
        out_specs=(VMEM,) * 4,
        scratch_shapes=[pltpu.VMEM((all_q, HD), jnp.float32)],
    )(cache_lengths, queries, cache_keys, cache_values)

    half = HD // 2
    inverse = jnp.asarray(ROPE_BASE ** (-2.0 * np.arange(half) / HD), jnp.float32)
    positions = (cache_lengths[:, None] + jnp.arange(step_count, dtype=jnp.int32)[None, :]).astype(jnp.float32)
    turns = positions.reshape(tokens, 1) * inverse[None, :]
    cosine, sine = jnp.cos(turns), jnp.sin(turns)
    cosine = jnp.concatenate([cosine, cosine], -1)
    sine = jnp.concatenate([-sine, sine], -1)


    square = jax.ShapeDtypeStruct((k_rows, col_width), jnp.float32)
    new_moment_one, new_moment_two, copies = pl.pallas_call(
        update_kernel,
        out_shape=(square, square, jax.ShapeDtypeStruct((ZH, k_rows, col_width), jnp.bfloat16)),
        in_specs=[VMEM] * 5,
        out_specs=(VMEM,) * 3,
    )(near(squares), near(grad_sum), near(master), near(moment_one), near(moment_two))
    rows_here = swapped(copies, ("zh",), [ORDER])
    cached, angles = (q_rows, old_acc, old_max, old_sum), (cosine, sine)
    rows_here, inputs, cached, angles = lax.optimization_barrier((rows_here, inputs, cached, angles))
    shares = jnp.dot(inputs, rows_here.reshape(ZH * k_rows, col_width), preferred_element_type=jnp.float32)
    parts = swapped(shares.reshape(n_split, tokens, col_width), SPLIT)

    entries, attended = pl.pallas_call(
        tail_kernel,
        out_shape=(
            jax.ShapeDtypeStruct((row_count, step_count, col_width), jnp.bfloat16),
            jax.ShapeDtypeStruct((row_count, step_count, GROUPS * HD), jnp.bfloat16),
        ),
        in_specs=[VMEM] * 7,
        out_specs=(VMEM,) * 2,
        scratch_shapes=[pltpu.VMEM((all_q, HD), jnp.float32), pltpu.VMEM((tokens, col_width), jnp.float32)],
    )(*[near(array) for array in (parts, *angles, *cached)])
    return (new_moment_one, new_moment_two, entries, attended)


def solution(mesh):
    torus = Mesh(mesh.devices.reshape(2, ZH, ZL, 2, 4, 2), ("g", "zh", "zl", "xl", "y", "c"))
    return jax.shard_map(
        body,
        mesh=torus,
        in_specs=(
            P(TP, GRP_REP, None),
            P(GRP_REP, TP),
            P(GRP_REP, TP),
            P(GRP_REP, TP),
            P(GRP_REP, None, None),
            P(GRP_REP, None, TP),
            P(GRP_REP, None, TP),
            P(GRP_REP, None, TP),
            P(GRP_REP),
        ),
        out_specs=(P(GRP_REP, TP), P(GRP_REP, TP), P(GRP_REP, None, TP), P(GRP_REP, None, TP)),
        check_vma=False,
    )
```

```python
import functools
import math

import jax
import jax.numpy as jnp
import numpy as np
from jax import lax
from jax.experimental import pallas as pl
from jax.experimental.pallas import tpu as pltpu
from jax.sharding import Mesh
from jax.sharding import PartitionSpec as P

D = 5120
QH = 40
KVH = 8
HD = 128
GROUPS = QH // KVH
ZH, ZL = 8, 4
TP = ("y", "c")
REP = ("zh", "zl", "xl")
GRP_REP = ("g",) + REP
SPLIT = ("zl", "g", "xl")
ORDER = tuple((i + 5) % ZH for i in range(ZH))
QROWS = 24

BETA_ONE = 0.9
BETA_TWO = 0.999
FIRST_CORR = 0.9999734386011124
SECOND_CORR = 0.09520785288629041
LEARN_RATE = 0.003
EPSILON = 1e-08
ROPE_BASE = 1000000.0
NEG_FILL = -1e30


def swapped(blocks, axes, groups=None):
    return lax.all_to_all(blocks, axes, split_axis=0, concat_axis=0, tiled=True, axis_index_groups=groups)


def near(array):
    return pltpu.with_memory_space_constraint(array, pltpu.VMEM)


def norm_kernel(parts_ref, x_ref, sum_ref, out_ref, flat_ref):
    total = parts_ref[0]
    for i in range(1, parts_ref.shape[0]):
        total = total + parts_ref[i]
    sum_ref[...] = total
    squares = jnp.sum(jnp.sum(total * total, axis=0, keepdims=True), axis=1, keepdims=True)
    high = squares.astype(jnp.bfloat16).astype(jnp.float32)
    rest = squares - high
    middle = rest.astype(jnp.bfloat16).astype(jnp.float32)
    low = rest - middle
    rows, steps, width = x_ref.shape
    for r in range(rows):
        flat_ref[pl.ds(r * steps, steps), :] = x_ref[r].astype(jnp.float32)
    step = width // (ZH * ZL * 4)
    row = lax.broadcasted_iota(jnp.int32, (rows * steps, out_ref.shape[2] - ZH * step), 0)
    terms = jnp.where(row == 0, high, jnp.where(row == 1, middle, jnp.where(row == 2, low, 0.0)))
    for zl in range(ZL):
        for x in range(4):
            cols = []
            for zh in ORDER:
                start = (((x // 2 * ZH + zh) * ZL + zl) * 2 + x % 2) * step
                cols.append(flat_ref[:, start : start + step])
            out_ref[zl * 4 + x] = jnp.concatenate(cols + [terms], axis=1).astype(jnp.bfloat16)


def share_kernel(blocks_ref, squares_ref, inputs_ref):
    n, tokens, _ = blocks_ref.shape
    depth = inputs_ref.shape[1]
    terms = blocks_ref[:, :, 256:384].astype(jnp.float32)
    total = jnp.sum(jnp.sum(terms, axis=0), axis=0, keepdims=True)
    total = jnp.broadcast_to(total[:, depth - 256 : depth - 255], (1, squares_ref.shape[2]))
    for i in range(squares_ref.shape[0]):
        squares_ref[i] = total
    inputs_ref[...] = blocks_ref[:, :, :depth].reshape(n * tokens, depth)


def update_kernel(squares_ref, sum_ref, master_ref, one_ref, two_ref, new_one_ref, new_two_ref, copies_ref):
    squares = jnp.sum(squares_ref[...], axis=0)
    scale = jnp.minimum(1.0, math.sqrt(D * 2 * KVH * HD) / jnp.sqrt(squares))[:, :1]
    clipped = sum_ref[...] * scale
    one = BETA_ONE * one_ref[...] + (1.0 - BETA_ONE) * clipped
    two = BETA_TWO * two_ref[...] + (1.0 - BETA_TWO) * clipped * clipped
    new_one_ref[...] = one
    new_two_ref[...] = two
    update = one / FIRST_CORR / (jnp.sqrt(two / SECOND_CORR) + EPSILON)
    weights = (master_ref[...] - LEARN_RATE * update).astype(jnp.bfloat16)
    for i in range(copies_ref.shape[0]):
        copies_ref[i] = weights


def cache_kernel(len_ref, q_ref, k_ref, v_ref, qs_ref, acc_ref, max_ref, sum_ref, qf_ref):
    rows, slots = k_ref.shape[0], k_ref.shape[1]
    steps = q_ref.shape[1]
    qf_ref[...] = jnp.zeros_like(qf_ref)
    for r in range(rows):
        q = q_ref[r].astype(jnp.float32)
        for h in range(GROUPS):
            qf_ref[pl.ds(r * QROWS + h * steps, steps), :] = q[:, h * HD : (h + 1) * HD]
    qs_ref[...] = qf_ref[...].astype(jnp.bfloat16)
    slot = lax.broadcasted_iota(jnp.int32, (QROWS, slots), 1)
    for r in range(rows):
        qb = qf_ref[pl.ds(r * QROWS, QROWS), :].astype(jnp.bfloat16)
        s = lax.dot_general(qb, k_ref[r], (((1,), (1,)), ((), ())), preferred_element_type=jnp.float32)
        s = jnp.where(slot < len_ref[r], s * (1.0 / math.sqrt(HD)), NEG_FILL)
        top = jnp.max(s, axis=1, keepdims=True)
        p = jnp.exp(s - top)
        total = jnp.sum(p, axis=1, keepdims=True)
        acc = jnp.dot(p.astype(jnp.bfloat16), v_ref[r], preferred_element_type=jnp.float32)
        at = pl.ds(r * QROWS, QROWS)
        acc_ref[at, :] = acc
        max_ref[at, :] = jnp.broadcast_to(top, (QROWS, HD))
        sum_ref[at, :] = jnp.broadcast_to(total, (QROWS, HD))


def tail_kernel(part_ref, cos_ref, sin_ref, q_ref, acc_ref, max_ref, sum_ref, new_ref, out_ref, o_ref, n_ref):
    tokens = part_ref.shape[1]
    rows, steps = out_ref.shape[0], out_ref.shape[1]
    projected = part_ref[0].astype(jnp.float32)
    for i in range(1, part_ref.shape[0]):
        projected = projected + part_ref[i].astype(jnp.float32)
    k, v = projected[:, :HD], projected[:, HD:]
    turned = pltpu.roll(k, HD // 2, 1)
    k = k * cos_ref[...] + turned * sin_ref[...]
    kb, vb = k.astype(jnp.bfloat16), v.astype(jnp.bfloat16)
    n_ref[:, :HD] = k
    n_ref[:, HD:] = v
    for r in range(rows):
        new_ref[r] = n_ref[pl.ds(r * steps, steps), :].astype(jnp.bfloat16)
    total_q = q_ref.shape[0]
    s = lax.dot_general(q_ref[...], kb, (((1,), (1,)), ((), ())), preferred_element_type=jnp.float32)
    s = s * (1.0 / math.sqrt(HD))
    q_at = lax.broadcasted_iota(jnp.int32, (total_q, tokens), 0)
    t_at = lax.broadcasted_iota(jnp.int32, (total_q, tokens), 1)
    ok = t_at < 0
    for r in range(rows):
        inside = (q_at >= r * QROWS) & (q_at < (r + 1) * QROWS) & (t_at >= r * steps)
        ok = ok | (inside & (t_at <= r * steps + (q_at & (steps - 1))))
    s = jnp.where(ok, s, NEG_FILL)
    top = jnp.maximum(jnp.max(s, axis=1, keepdims=True), max_ref[...])
    p = jnp.where(ok, jnp.exp(s - top[:, :1]), 0.0)
    fade = jnp.exp(max_ref[...] - top)
    total = sum_ref[...] * fade + jnp.sum(p, axis=1, keepdims=True)
    acc = acc_ref[...] * fade + jnp.dot(p.astype(jnp.bfloat16), vb, preferred_element_type=jnp.float32)
    o_ref[...] = acc / total
    for r in range(rows):
        for h in range(GROUPS):
            out_ref[r, :, h * HD : (h + 1) * HD] = o_ref[pl.ds(r * QROWS + h * steps, steps), :].astype(jnp.bfloat16)


VMEM = pl.BlockSpec(memory_space=pltpu.VMEM)
SMEM = pl.BlockSpec(memory_space=pltpu.SMEM)


def body(grad_parts, master, moment_one, moment_two, hidden_in, queries, cache_keys, cache_values, cache_lengths):
    k_rows, col_width = master.shape
    row_count, step_count, model_width = hidden_in.shape
    tokens = row_count * step_count
    n_split = 4 * ZL
    n_tp = 8
    depth = model_width // n_split
    all_q = row_count * QROWS

    tiles = jnp.moveaxis(grad_parts[0].reshape(k_rows, n_tp, col_width), 1, 0)
    arrived = swapped(tiles, TP)
    grad_sum, blocks = pl.pallas_call(
        norm_kernel,
        out_shape=(
            jax.ShapeDtypeStruct((k_rows, col_width), jnp.float32),
            jax.ShapeDtypeStruct((n_split, tokens, depth + 64), jnp.bfloat16),
        ),
        in_specs=[VMEM] * 2,
        out_specs=(VMEM,) * 2,
        scratch_shapes=[pltpu.VMEM((tokens, model_width), jnp.float32)],
    )(near(arrived), near(hidden_in))
    squares, inputs = pl.pallas_call(
        share_kernel,
        out_shape=(
            jax.ShapeDtypeStruct((ZH * n_tp, 1, HD), jnp.float32),
            jax.ShapeDtypeStruct((n_split * tokens, depth), jnp.bfloat16),
        ),
        in_specs=[VMEM],
        out_specs=(VMEM,) * 2,
    )(near(swapped(blocks, SPLIT)))
    inputs, squares, cache_lengths = lax.optimization_barrier((inputs, squares, cache_lengths))
    peers = [zh * n_tp + t for zh in ORDER for t in range(n_tp)]
    squares = swapped(squares, ("zh",) + TP, [peers])

    q_rows, old_acc, old_max, old_sum = pl.pallas_call(
        cache_kernel,
        out_shape=(
            jax.ShapeDtypeStruct((all_q, HD), jnp.bfloat16),
            jax.ShapeDtypeStruct((all_q, HD), jnp.float32),
            jax.ShapeDtypeStruct((all_q, HD), jnp.float32),
            jax.ShapeDtypeStruct((all_q, HD), jnp.float32),
        ),
        in_specs=[SMEM, VMEM, VMEM, VMEM],
        out_specs=(VMEM,) * 4,
        scratch_shapes=[pltpu.VMEM((all_q, HD), jnp.float32)],
    )(cache_lengths, queries, cache_keys, cache_values)

    half = HD // 2
    inverse = jnp.asarray(ROPE_BASE ** (-2.0 * np.arange(half) / HD), jnp.float32)
    positions = (cache_lengths[:, None] + jnp.arange(step_count, dtype=jnp.int32)[None, :]).astype(jnp.float32)
    turns = positions.reshape(tokens, 1) * inverse[None, :]
    cosine, sine = jnp.cos(turns), jnp.sin(turns)
    cosine = jnp.concatenate([cosine, cosine], -1)
    sine = jnp.concatenate([-sine, sine], -1)


    square = jax.ShapeDtypeStruct((k_rows, col_width), jnp.float32)
    new_moment_one, new_moment_two, copies = pl.pallas_call(
        update_kernel,
        out_shape=(square, square, jax.ShapeDtypeStruct((ZH, k_rows, col_width), jnp.bfloat16)),
        in_specs=[VMEM] * 5,
        out_specs=(VMEM,) * 3,
    )(near(squares), near(grad_sum), near(master), near(moment_one), near(moment_two))
    rows_here = swapped(copies, ("zh",), [ORDER])
    cached, angles = (q_rows, old_acc, old_max, old_sum), (cosine, sine)
    rows_here, inputs, cached, angles = lax.optimization_barrier((rows_here, inputs, cached, angles))
    shares = jnp.dot(inputs, rows_here.reshape(ZH * k_rows, col_width), preferred_element_type=jnp.float32)
    parts = swapped(shares.reshape(n_split, tokens, col_width), SPLIT)

    entries, attended = pl.pallas_call(
        tail_kernel,
        out_shape=(
            jax.ShapeDtypeStruct((row_count, step_count, col_width), jnp.bfloat16),
            jax.ShapeDtypeStruct((row_count, step_count, GROUPS * HD), jnp.bfloat16),
        ),
        in_specs=[VMEM] * 7,
        out_specs=(VMEM,) * 2,
        scratch_shapes=[pltpu.VMEM((all_q, HD), jnp.float32), pltpu.VMEM((tokens, col_width), jnp.float32)],
    )(*[near(array) for array in (parts, *angles, *cached)])
    return (new_moment_one, new_moment_two, entries, attended)


def solution(mesh):
    torus = Mesh(mesh.devices.reshape(2, ZH, ZL, 2, 4, 2), ("g", "zh", "zl", "xl", "y", "c"))
    return jax.shard_map(
        body,
        mesh=torus,
        in_specs=(
            P(TP, GRP_REP, None),
            P(GRP_REP, TP),
            P(GRP_REP, TP),
            P(GRP_REP, TP),
            P(GRP_REP, None, None),
            P(GRP_REP, None, TP),
            P(GRP_REP, None, TP),
            P(GRP_REP, None, TP),
            P(GRP_REP),
        ),
        out_specs=(P(GRP_REP, TP), P(GRP_REP, TP), P(GRP_REP, None, TP), P(GRP_REP, None, TP)),
        check_vma=False,
    )
```

```python
import functools
import math

import jax
import jax.numpy as jnp
import numpy as np
from jax import lax
from jax.experimental import pallas as pl
from jax.experimental.pallas import tpu as pltpu
from jax.sharding import Mesh
from jax.sharding import PartitionSpec as P

D = 5120
QH = 40
KVH = 8
HD = 128
GROUPS = QH // KVH
ZH, ZL = 8, 4
TP = ("y", "c")
REP = ("zh", "zl", "xl")
GRP_REP = ("g",) + REP
SPLIT = ("zl", "g", "xl")
ORDER = (5, 4, 0, 1, 2, 6, 7, 3)
NORM_ORDER = tuple(zh * 8 + t for zh in ORDER for t in range(8))
SPLIT_ORDER = tuple(range(15, -1, -1))
QROWS = 24

BETA_ONE = 0.9
BETA_TWO = 0.999
FIRST_CORR = 0.9999734386011124
SECOND_CORR = 0.09520785288629041
LEARN_RATE = 0.003
EPSILON = 1e-08
ROPE_BASE = 1000000.0
NEG_FILL = -1e30


def swapped(blocks, axes, groups=None):
    return lax.all_to_all(blocks, axes, split_axis=0, concat_axis=0, tiled=True, axis_index_groups=groups)


def near(array):
    return pltpu.with_memory_space_constraint(array, pltpu.VMEM)


def norm_kernel(parts_ref, x_ref, sum_ref, out_ref, flat_ref):
    total = parts_ref[0]
    for i in range(1, parts_ref.shape[0]):
        total = total + parts_ref[i]
    sum_ref[...] = total
    squares = jnp.sum(jnp.sum(total * total, axis=0, keepdims=True), axis=1, keepdims=True)
    high = squares.astype(jnp.bfloat16).astype(jnp.float32)
    rest = squares - high
    middle = rest.astype(jnp.bfloat16).astype(jnp.float32)
    low = rest - middle
    rows, steps, width = x_ref.shape
    for r in range(rows):
        flat_ref[pl.ds(r * steps, steps), :] = x_ref[r].astype(jnp.float32)
    step = width // (ZH * ZL * 4)
    row = lax.broadcasted_iota(jnp.int32, (rows * steps, out_ref.shape[2] - ZH * step), 0)
    terms = jnp.where(row == 0, high, jnp.where(row == 1, middle, jnp.where(row == 2, low, 0.0)))
    for zl in range(ZL):
        for x in range(4):
            cols = []
            for zh in ORDER:
                start = (((x // 2 * ZH + zh) * ZL + zl) * 2 + x % 2) * step
                cols.append(flat_ref[:, start : start + step])
            out_ref[SPLIT_ORDER.index(zl * 4 + x)] = jnp.concatenate(cols + [terms], axis=1).astype(jnp.bfloat16)


def share_kernel(blocks_ref, squares_ref, inputs_ref):
    n, tokens, _ = blocks_ref.shape
    depth = inputs_ref.shape[1]
    terms = blocks_ref[:, :, 256:384].astype(jnp.float32)
    total = jnp.sum(jnp.sum(terms, axis=0), axis=0, keepdims=True)
    total = jnp.broadcast_to(total[:, depth - 256 : depth - 255], (1, squares_ref.shape[2]))
    for i in range(squares_ref.shape[0]):
        squares_ref[i] = total
    inputs_ref[...] = blocks_ref[:, :, :depth].reshape(n * tokens, depth)


def update_kernel(squares_ref, sum_ref, master_ref, one_ref, two_ref, new_one_ref, new_two_ref, copies_ref):
    squares = jnp.sum(squares_ref[...], axis=0)
    scale = jnp.minimum(1.0, math.sqrt(D * 2 * KVH * HD) / jnp.sqrt(squares))[:, :1]
    clipped = sum_ref[...] * scale
    one = BETA_ONE * one_ref[...] + (1.0 - BETA_ONE) * clipped
    two = BETA_TWO * two_ref[...] + (1.0 - BETA_TWO) * clipped * clipped
    new_one_ref[...] = one
    new_two_ref[...] = two
    update = one / FIRST_CORR / (jnp.sqrt(two / SECOND_CORR) + EPSILON)
    weights = (master_ref[...] - LEARN_RATE * update).astype(jnp.bfloat16)
    for i in range(copies_ref.shape[0]):
        copies_ref[i] = weights


def cache_kernel(len_ref, q_ref, k_ref, v_ref, qs_ref, acc_ref, max_ref, sum_ref, qf_ref):
    rows, slots = k_ref.shape[0], k_ref.shape[1]
    steps = q_ref.shape[1]
    qf_ref[...] = jnp.zeros_like(qf_ref)
    for r in range(rows):
        q = q_ref[r].astype(jnp.float32)
        for h in range(GROUPS):
            qf_ref[pl.ds(r * QROWS + h * steps, steps), :] = q[:, h * HD : (h + 1) * HD]
    qs_ref[...] = qf_ref[...].astype(jnp.bfloat16)
    slot = lax.broadcasted_iota(jnp.int32, (QROWS, slots), 1)
    for r in range(rows):
        qb = qf_ref[pl.ds(r * QROWS, QROWS), :].astype(jnp.bfloat16)
        s = lax.dot_general(qb, k_ref[r], (((1,), (1,)), ((), ())), preferred_element_type=jnp.float32)
        s = jnp.where(slot < len_ref[r], s * (1.0 / math.sqrt(HD)), NEG_FILL)
        top = jnp.max(s, axis=1, keepdims=True)
        p = jnp.exp(s - top)
        total = jnp.sum(p, axis=1, keepdims=True)
        acc = jnp.dot(p.astype(jnp.bfloat16), v_ref[r], preferred_element_type=jnp.float32)
        at = pl.ds(r * QROWS, QROWS)
        acc_ref[at, :] = acc
        max_ref[at, :] = jnp.broadcast_to(top, (QROWS, HD))
        sum_ref[at, :] = jnp.broadcast_to(total, (QROWS, HD))


def tail_kernel(part_ref, cos_ref, sin_ref, q_ref, acc_ref, max_ref, sum_ref, new_ref, out_ref, o_ref, n_ref):
    tokens = part_ref.shape[1]
    rows, steps = out_ref.shape[0], out_ref.shape[1]
    projected = part_ref[0].astype(jnp.float32)
    for i in range(1, part_ref.shape[0]):
        projected = projected + part_ref[i].astype(jnp.float32)
    k, v = projected[:, :HD], projected[:, HD:]
    turned = pltpu.roll(k, HD // 2, 1)
    k = k * cos_ref[...] + turned * sin_ref[...]
    kb, vb = k.astype(jnp.bfloat16), v.astype(jnp.bfloat16)
    n_ref[:, :HD] = k
    n_ref[:, HD:] = v
    for r in range(rows):
        new_ref[r] = n_ref[pl.ds(r * steps, steps), :].astype(jnp.bfloat16)
    total_q = q_ref.shape[0]
    s = lax.dot_general(q_ref[...], kb, (((1,), (1,)), ((), ())), preferred_element_type=jnp.float32)
    s = s * (1.0 / math.sqrt(HD))
    q_at = lax.broadcasted_iota(jnp.int32, (total_q, tokens), 0)
    t_at = lax.broadcasted_iota(jnp.int32, (total_q, tokens), 1)
    ok = t_at < 0
    for r in range(rows):
        inside = (q_at >= r * QROWS) & (q_at < (r + 1) * QROWS) & (t_at >= r * steps)
        ok = ok | (inside & (t_at <= r * steps + (q_at & (steps - 1))))
    s = jnp.where(ok, s, NEG_FILL)
    top = jnp.maximum(jnp.max(s, axis=1, keepdims=True), max_ref[...])
    p = jnp.where(ok, jnp.exp(s - top[:, :1]), 0.0)
    fade = jnp.exp(max_ref[...] - top)
    total = sum_ref[...] * fade + jnp.sum(p, axis=1, keepdims=True)
    acc = acc_ref[...] * fade + jnp.dot(p.astype(jnp.bfloat16), vb, preferred_element_type=jnp.float32)
    o_ref[...] = acc / total
    for r in range(rows):
        for h in range(GROUPS):
            out_ref[r, :, h * HD : (h + 1) * HD] = o_ref[pl.ds(r * QROWS + h * steps, steps), :].astype(jnp.bfloat16)


VMEM = pl.BlockSpec(memory_space=pltpu.VMEM)
SMEM = pl.BlockSpec(memory_space=pltpu.SMEM)


def body(grad_parts, master, moment_one, moment_two, hidden_in, queries, cache_keys, cache_values, cache_lengths):
    k_rows, col_width = master.shape
    row_count, step_count, model_width = hidden_in.shape
    tokens = row_count * step_count
    n_split = 4 * ZL
    n_tp = 8
    depth = model_width // n_split
    all_q = row_count * QROWS

    tiles = jnp.moveaxis(grad_parts[0].reshape(k_rows, n_tp, col_width), 1, 0)
    arrived = swapped(tiles, TP)
    grad_sum, blocks = pl.pallas_call(
        norm_kernel,
        out_shape=(
            jax.ShapeDtypeStruct((k_rows, col_width), jnp.float32),
            jax.ShapeDtypeStruct((n_split, tokens, depth + 64), jnp.bfloat16),
        ),
        in_specs=[VMEM] * 2,
        out_specs=(VMEM,) * 2,
        scratch_shapes=[pltpu.VMEM((tokens, model_width), jnp.float32)],
    )(near(arrived), near(hidden_in))
    squares, inputs = pl.pallas_call(
        share_kernel,
        out_shape=(
            jax.ShapeDtypeStruct((ZH * n_tp, 1, HD), jnp.float32),
            jax.ShapeDtypeStruct((n_split * tokens, depth), jnp.bfloat16),
        ),
        in_specs=[VMEM],
        out_specs=(VMEM,) * 2,
    )(near(swapped(blocks, SPLIT, [SPLIT_ORDER])))
    inputs, squares, cache_lengths = lax.optimization_barrier((inputs, squares, cache_lengths))
    squares = swapped(squares, ("zh",) + TP, [NORM_ORDER])

    q_rows, old_acc, old_max, old_sum = pl.pallas_call(
        cache_kernel,
        out_shape=(
            jax.ShapeDtypeStruct((all_q, HD), jnp.bfloat16),
            jax.ShapeDtypeStruct((all_q, HD), jnp.float32),
            jax.ShapeDtypeStruct((all_q, HD), jnp.float32),
            jax.ShapeDtypeStruct((all_q, HD), jnp.float32),
        ),
        in_specs=[SMEM, VMEM, VMEM, VMEM],
        out_specs=(VMEM,) * 4,
        scratch_shapes=[pltpu.VMEM((all_q, HD), jnp.float32)],
    )(cache_lengths, queries, cache_keys, cache_values)

    half = HD // 2
    inverse = jnp.asarray(ROPE_BASE ** (-2.0 * np.arange(half) / HD), jnp.float32)
    positions = (cache_lengths[:, None] + jnp.arange(step_count, dtype=jnp.int32)[None, :]).astype(jnp.float32)
    turns = positions.reshape(tokens, 1) * inverse[None, :]
    cosine, sine = jnp.cos(turns), jnp.sin(turns)
    cosine = jnp.concatenate([cosine, cosine], -1)
    sine = jnp.concatenate([-sine, sine], -1)


    square = jax.ShapeDtypeStruct((k_rows, col_width), jnp.float32)
    new_moment_one, new_moment_two, copies = pl.pallas_call(
        update_kernel,
        out_shape=(square, square, jax.ShapeDtypeStruct((ZH, k_rows, col_width), jnp.bfloat16)),
        in_specs=[VMEM] * 5,
        out_specs=(VMEM,) * 3,
    )(near(squares), near(grad_sum), near(master), near(moment_one), near(moment_two))
    rows_here = swapped(copies, ("zh",), [ORDER])
    cached, angles = (q_rows, old_acc, old_max, old_sum), (cosine, sine)
    rows_here, inputs, cached, angles = lax.optimization_barrier((rows_here, inputs, cached, angles))
    shares = jnp.dot(inputs, rows_here.reshape(ZH * k_rows, col_width), preferred_element_type=jnp.float32)
    parts = swapped(shares.reshape(n_split, tokens, col_width), SPLIT, [SPLIT_ORDER])

    entries, attended = pl.pallas_call(
        tail_kernel,
        out_shape=(
            jax.ShapeDtypeStruct((row_count, step_count, col_width), jnp.bfloat16),
            jax.ShapeDtypeStruct((row_count, step_count, GROUPS * HD), jnp.bfloat16),
        ),
        in_specs=[VMEM] * 7,
        out_specs=(VMEM,) * 2,
        scratch_shapes=[pltpu.VMEM((all_q, HD), jnp.float32), pltpu.VMEM((tokens, col_width), jnp.float32)],
    )(*[near(array) for array in (parts, *angles, *cached)])
    return (new_moment_one, new_moment_two, entries, attended)


def solution(mesh):
    torus = Mesh(mesh.devices.reshape(2, ZH, ZL, 2, 4, 2), ("g", "zh", "zl", "xl", "y", "c"))
    return jax.shard_map(
        body,
        mesh=torus,
        in_specs=(
            P(TP, GRP_REP, None),
            P(GRP_REP, TP),
            P(GRP_REP, TP),
            P(GRP_REP, TP),
            P(GRP_REP, None, None),
            P(GRP_REP, None, TP),
            P(GRP_REP, None, TP),
            P(GRP_REP, None, TP),
            P(GRP_REP),
        ),
        out_specs=(P(GRP_REP, TP), P(GRP_REP, TP), P(GRP_REP, None, TP), P(GRP_REP, None, TP)),
        check_vma=False,
    )
```

```python
import functools
import math

import jax
import jax.numpy as jnp
import numpy as np
from jax import lax
from jax.experimental import pallas as pl
from jax.experimental.pallas import tpu as pltpu
from jax.sharding import Mesh
from jax.sharding import PartitionSpec as P

D = 5120
QH = 40
KVH = 8
HD = 128
GROUPS = QH // KVH
ZH, ZL = 8, 4
TP = ("y", "c")
REP = ("zh", "zl", "xl")
GRP_REP = ("g",) + REP
SPLIT = ("zl", "g", "xl")
ORDER = (5, 4, 0, 1, 2, 6, 7, 3)
SPLIT_ORDER = tuple(range(15, -1, -1))
SPLIT_CORE_ORDER = tuple(s * 2 + c for s in SPLIT_ORDER for c in range(2))
NORM_ORDER = tuple(zh * 4 + y for zh in ORDER for y in range(4))
QROWS = 24

BETA_ONE = 0.9
BETA_TWO = 0.999
FIRST_CORR = 0.9999734386011124
SECOND_CORR = 0.09520785288629041
LEARN_RATE = 0.003
EPSILON = 1e-08
ROPE_BASE = 1000000.0
NEG_FILL = -1e30


def swapped(blocks, axes, groups=None):
    return lax.all_to_all(blocks, axes, split_axis=0, concat_axis=0, tiled=True, axis_index_groups=groups)


def near(array):
    return pltpu.with_memory_space_constraint(array, pltpu.VMEM)


def norm_kernel(parts_ref, x_ref, sum_ref, out_ref, flat_ref):
    total = parts_ref[0]
    for i in range(1, parts_ref.shape[0]):
        total = total + parts_ref[i]
    sum_ref[...] = total
    squares = jnp.sum(jnp.sum(total * total, axis=0, keepdims=True), axis=1, keepdims=True)
    high = squares.astype(jnp.bfloat16).astype(jnp.float32)
    rest = squares - high
    middle = rest.astype(jnp.bfloat16).astype(jnp.float32)
    low = rest - middle
    cores, width, steps = 2, x_ref.shape[2], x_ref.shape[1]
    share = x_ref.shape[0] // cores
    for r in range(share):
        flat_ref[pl.ds(r * steps, steps), :] = x_ref[lax.axis_index("c") * share + r].astype(jnp.float32)
    step = width // (ZH * ZL * 4)
    room = (out_ref.shape[1], out_ref.shape[2] - ZH * step)
    row, lane = lax.broadcasted_iota(jnp.int32, room, 0), lax.broadcasted_iota(jnp.int32, room, 1)
    terms = jnp.where(lane == 0, high, jnp.where(lane == 1, middle, jnp.where(lane == 2, low, 0.0)))
    terms = jnp.where(row == 0, terms, 0.0)
    for zl in range(ZL):
        for x in range(4):
            cols = []
            for zh in ORDER:
                start = (((x // 2 * ZH + zh) * ZL + zl) * 2 + x % 2) * step
                cols.append(flat_ref[:, start : start + step])
            block = jnp.concatenate(cols + [terms], axis=1).astype(jnp.bfloat16)
            for c in range(cores):
                out_ref[SPLIT_ORDER.index(zl * 4 + x) * cores + c] = block


def share_kernel(blocks_ref, squares_ref, *, depth):
    first = depth // HD * HD
    terms = jnp.sum(blocks_ref[:, :, first : first + HD].astype(jnp.float32), axis=0)[:1, depth - first :]
    total = terms[:, :1] + (terms[:, 1:2] + terms[:, 2:3])
    for i in range(squares_ref.shape[0]):
        squares_ref[i] = jnp.broadcast_to(total, squares_ref.shape[1:])


def update_kernel(squares_ref, sum_ref, master_ref, one_ref, two_ref, new_one_ref, new_two_ref, copies_ref):
    squares = jnp.sum(squares_ref[...], axis=0)
    scale = jnp.minimum(1.0, math.sqrt(D * 2 * KVH * HD) / jnp.sqrt(squares))[:, :1]
    clipped = sum_ref[...] * scale
    one = BETA_ONE * one_ref[...] + (1.0 - BETA_ONE) * clipped
    two = BETA_TWO * two_ref[...] + (1.0 - BETA_TWO) * clipped * clipped
    new_one_ref[...] = one
    new_two_ref[...] = two
    update = one / FIRST_CORR / (jnp.sqrt(two / SECOND_CORR) + EPSILON)
    weights = (master_ref[...] - LEARN_RATE * update).astype(jnp.bfloat16)
    for i in range(copies_ref.shape[0]):
        copies_ref[i] = weights


def cache_kernel(len_ref, q_ref, k_ref, v_ref, qs_ref, acc_ref, max_ref, sum_ref, qf_ref):
    rows, slots = k_ref.shape[0], k_ref.shape[1]
    steps = q_ref.shape[1]
    qf_ref[...] = jnp.zeros_like(qf_ref)
    for r in range(rows):
        q = q_ref[r].astype(jnp.float32)
        for h in range(GROUPS):
            qf_ref[pl.ds(r * QROWS + h * steps, steps), :] = q[:, h * HD : (h + 1) * HD]
    qs_ref[...] = qf_ref[...].astype(jnp.bfloat16)
    slot = lax.broadcasted_iota(jnp.int32, (QROWS, slots), 1)
    for r in range(rows):
        qb = qf_ref[pl.ds(r * QROWS, QROWS), :].astype(jnp.bfloat16)
        s = lax.dot_general(qb, k_ref[r], (((1,), (1,)), ((), ())), preferred_element_type=jnp.float32)
        s = jnp.where(slot < len_ref[r], s * (1.0 / math.sqrt(HD)), NEG_FILL)
        top = jnp.max(s, axis=1, keepdims=True)
        p = jnp.exp(s - top)
        total = jnp.sum(p, axis=1, keepdims=True)
        acc = jnp.dot(p.astype(jnp.bfloat16), v_ref[r], preferred_element_type=jnp.float32)
        at = pl.ds(r * QROWS, QROWS)
        acc_ref[at, :] = acc
        max_ref[at, :] = jnp.broadcast_to(top, (QROWS, HD))
        sum_ref[at, :] = jnp.broadcast_to(total, (QROWS, HD))


def tail_kernel(part_ref, cos_ref, sin_ref, q_ref, acc_ref, max_ref, sum_ref, new_ref, out_ref, o_ref, n_ref):
    tokens = part_ref.shape[1]
    rows, steps = out_ref.shape[0], out_ref.shape[1]
    projected = part_ref[0].astype(jnp.float32)
    for i in range(1, part_ref.shape[0]):
        projected = projected + part_ref[i].astype(jnp.float32)
    k, v = projected[:, :HD], projected[:, HD:]
    turned = pltpu.roll(k, HD // 2, 1)
    k = k * cos_ref[...] + turned * sin_ref[...]
    kb, vb = k.astype(jnp.bfloat16), v.astype(jnp.bfloat16)
    n_ref[:, :HD] = k
    n_ref[:, HD:] = v
    for r in range(rows):
        new_ref[r] = n_ref[pl.ds(r * steps, steps), :].astype(jnp.bfloat16)
    total_q = q_ref.shape[0]
    s = lax.dot_general(q_ref[...], kb, (((1,), (1,)), ((), ())), preferred_element_type=jnp.float32)
    s = s * (1.0 / math.sqrt(HD))
    q_at = lax.broadcasted_iota(jnp.int32, (total_q, tokens), 0)
    t_at = lax.broadcasted_iota(jnp.int32, (total_q, tokens), 1)
    ok = t_at < 0
    for r in range(rows):
        inside = (q_at >= r * QROWS) & (q_at < (r + 1) * QROWS) & (t_at >= r * steps)
        ok = ok | (inside & (t_at <= r * steps + (q_at & (steps - 1))))
    s = jnp.where(ok, s, NEG_FILL)
    top = jnp.maximum(jnp.max(s, axis=1, keepdims=True), max_ref[...])
    p = jnp.where(ok, jnp.exp(s - top[:, :1]), 0.0)
    fade = jnp.exp(max_ref[...] - top)
    total = sum_ref[...] * fade + jnp.sum(p, axis=1, keepdims=True)
    acc = acc_ref[...] * fade + jnp.dot(p.astype(jnp.bfloat16), vb, preferred_element_type=jnp.float32)
    o_ref[...] = acc / total
    for r in range(rows):
        for h in range(GROUPS):
            out_ref[r, :, h * HD : (h + 1) * HD] = o_ref[pl.ds(r * QROWS + h * steps, steps), :].astype(jnp.bfloat16)


VMEM = pl.BlockSpec(memory_space=pltpu.VMEM)
SMEM = pl.BlockSpec(memory_space=pltpu.SMEM)


def body(grad_parts, master, moment_one, moment_two, hidden_in, queries, cache_keys, cache_values, cache_lengths):
    k_rows, col_width = master.shape
    row_count, step_count, model_width = hidden_in.shape
    tokens = row_count * step_count
    n_split = 4 * ZL
    n_tp = 8
    depth = model_width // n_split
    all_q = row_count * QROWS

    tiles = jnp.moveaxis(grad_parts[0].reshape(k_rows, n_tp, col_width), 1, 0)
    arrived = swapped(tiles, TP)
    grad_sum, blocks = pl.pallas_call(
        norm_kernel,
        out_shape=(
            jax.ShapeDtypeStruct((k_rows, col_width), jnp.float32),
            jax.ShapeDtypeStruct((n_split * 2, tokens // 2, depth + 64), jnp.bfloat16),
        ),
        in_specs=[VMEM] * 2,
        out_specs=(VMEM,) * 2,
        scratch_shapes=[pltpu.VMEM((tokens // 2, model_width), jnp.float32)],
    )(near(arrived), near(hidden_in))
    blocks = swapped(blocks, SPLIT + ("c",), [SPLIT_CORE_ORDER])
    squares = pl.pallas_call(
        functools.partial(share_kernel, depth=depth),
        out_shape=jax.ShapeDtypeStruct((ZH * 4, 1, HD), jnp.float32),
        in_specs=[VMEM],
        out_specs=VMEM,
    )(near(blocks))
    blocks, squares, cache_lengths = lax.optimization_barrier((blocks, squares, cache_lengths))
    inputs = blocks[:, :, :depth].reshape(n_split * tokens, depth)
    squares = swapped(squares, ("zh", "y"), [NORM_ORDER])

    q_rows, old_acc, old_max, old_sum = pl.pallas_call(
        cache_kernel,
        out_shape=(
            jax.ShapeDtypeStruct((all_q, HD), jnp.bfloat16),
            jax.ShapeDtypeStruct((all_q, HD), jnp.float32),
            jax.ShapeDtypeStruct((all_q, HD), jnp.float32),
            jax.ShapeDtypeStruct((all_q, HD), jnp.float32),
        ),
        in_specs=[SMEM, VMEM, VMEM, VMEM],
        out_specs=(VMEM,) * 4,
        scratch_shapes=[pltpu.VMEM((all_q, HD), jnp.float32)],
    )(cache_lengths, queries, cache_keys, cache_values)

    half = HD // 2
    inverse = jnp.asarray(ROPE_BASE ** (-2.0 * np.arange(half) / HD), jnp.float32)
    positions = (cache_lengths[:, None] + jnp.arange(step_count, dtype=jnp.int32)[None, :]).astype(jnp.float32)
    turns = positions.reshape(tokens, 1) * inverse[None, :]
    cosine, sine = jnp.cos(turns), jnp.sin(turns)
    cosine = jnp.concatenate([cosine, cosine], -1)
    sine = jnp.concatenate([-sine, sine], -1)


    square = jax.ShapeDtypeStruct((k_rows, col_width), jnp.float32)
    new_moment_one, new_moment_two, copies = pl.pallas_call(
        update_kernel,
        out_shape=(square, square, jax.ShapeDtypeStruct((ZH, k_rows, col_width), jnp.bfloat16)),
        in_specs=[VMEM] * 5,
        out_specs=(VMEM,) * 3,
    )(near(squares), near(grad_sum), near(master), near(moment_one), near(moment_two))
    rows_here = swapped(copies, ("zh",), [ORDER])
    cached, angles = (q_rows, old_acc, old_max, old_sum), (cosine, sine)
    rows_here, inputs, cached, angles = lax.optimization_barrier((rows_here, inputs, cached, angles))
    shares = jnp.dot(inputs, rows_here.reshape(ZH * k_rows, col_width), preferred_element_type=jnp.float32)
    parts = swapped(shares.reshape(n_split, tokens, col_width), SPLIT, [SPLIT_ORDER])

    entries, attended = pl.pallas_call(
        tail_kernel,
        out_shape=(
            jax.ShapeDtypeStruct((row_count, step_count, col_width), jnp.bfloat16),
            jax.ShapeDtypeStruct((row_count, step_count, GROUPS * HD), jnp.bfloat16),
        ),
        in_specs=[VMEM] * 7,
        out_specs=(VMEM,) * 2,
        scratch_shapes=[pltpu.VMEM((all_q, HD), jnp.float32), pltpu.VMEM((tokens, col_width), jnp.float32)],
    )(*[near(array) for array in (parts, *angles, *cached)])
    return (new_moment_one, new_moment_two, entries, attended)


def solution(mesh):
    torus = Mesh(mesh.devices.reshape(2, ZH, ZL, 2, 4, 2), ("g", "zh", "zl", "xl", "y", "c"))
    return jax.shard_map(
        body,
        mesh=torus,
        in_specs=(
            P(TP, GRP_REP, None),
            P(GRP_REP, TP),
            P(GRP_REP, TP),
            P(GRP_REP, TP),
            P(GRP_REP, None, None),
            P(GRP_REP, None, TP),
            P(GRP_REP, None, TP),
            P(GRP_REP, None, TP),
            P(GRP_REP),
        ),
        out_specs=(P(GRP_REP, TP), P(GRP_REP, TP), P(GRP_REP, None, TP), P(GRP_REP, None, TP)),
        check_vma=False,
    )
```

```python
import functools
import math

import jax
import jax.numpy as jnp
import numpy as np
from jax import lax
from jax.experimental import pallas as pl
from jax.experimental.pallas import tpu as pltpu
from jax.sharding import Mesh
from jax.sharding import PartitionSpec as P

D = 5120
QH = 40
KVH = 8
HD = 128
GROUPS = QH // KVH
ZH, ZL = 8, 4
TP = ("y", "c")
REP = ("zh", "zl", "xl")
GRP_REP = ("g",) + REP
SPLIT = ("zl", "g", "xl")
ORDER = (5, 4, 0, 2, 1, 6, 7, 3)
SPLIT_ORDER = tuple(range(15, -1, -1))
SPLIT_CORE_ORDER = tuple(s * 2 + c for s in SPLIT_ORDER for c in range(2))
NORM_ORDER = tuple(zh * 4 + y for zh in ORDER for y in range(4))
QROWS = 24

BETA_ONE = 0.9
BETA_TWO = 0.999
FIRST_CORR = 0.9999734386011124
SECOND_CORR = 0.09520785288629041
LEARN_RATE = 0.003
EPSILON = 1e-08
ROPE_BASE = 1000000.0
NEG_FILL = -1e30


def swapped(blocks, axes, groups=None):
    return lax.all_to_all(blocks, axes, split_axis=0, concat_axis=0, tiled=True, axis_index_groups=groups)


def near(array):
    return pltpu.with_memory_space_constraint(array, pltpu.VMEM)


def norm_kernel(parts_ref, x_ref, sum_ref, out_ref, flat_ref):
    total = parts_ref[0]
    for i in range(1, parts_ref.shape[0]):
        total = total + parts_ref[i]
    sum_ref[...] = total
    squares = jnp.sum(jnp.sum(total * total, axis=0, keepdims=True), axis=1, keepdims=True)
    high = squares.astype(jnp.bfloat16).astype(jnp.float32)
    rest = squares - high
    middle = rest.astype(jnp.bfloat16).astype(jnp.float32)
    low = rest - middle
    cores, width, steps = 2, x_ref.shape[2], x_ref.shape[1]
    share = x_ref.shape[0] // cores
    for r in range(share):
        flat_ref[pl.ds(r * steps, steps), :] = x_ref[lax.axis_index("c") * share + r].astype(jnp.float32)
    step = width // (ZH * ZL * 4)
    room = (out_ref.shape[1], out_ref.shape[2] - ZH * step)
    row, lane = lax.broadcasted_iota(jnp.int32, room, 0), lax.broadcasted_iota(jnp.int32, room, 1)
    terms = jnp.where(lane == 0, high, jnp.where(lane == 1, middle, jnp.where(lane == 2, low, 0.0)))
    terms = jnp.where(row == 0, terms, 0.0)
    for zl in range(ZL):
        for x in range(4):
            cols = []
            for zh in ORDER:
                start = (((x // 2 * ZH + zh) * ZL + zl) * 2 + x % 2) * step
                cols.append(flat_ref[:, start : start + step])
            block = jnp.concatenate(cols + [terms], axis=1).astype(jnp.bfloat16)
            for c in range(cores):
                out_ref[SPLIT_ORDER.index(zl * 4 + x) * cores + c] = block


def share_kernel(blocks_ref, squares_ref, *, depth):
    first = depth // HD * HD
    terms = jnp.sum(blocks_ref[:, :, first : first + HD].astype(jnp.float32), axis=0)[:1, depth - first :]
    total = terms[:, :1] + (terms[:, 1:2] + terms[:, 2:3])
    for i in range(squares_ref.shape[0]):
        squares_ref[i] = jnp.broadcast_to(total, squares_ref.shape[1:])


def update_kernel(squares_ref, sum_ref, master_ref, one_ref, two_ref, new_one_ref, new_two_ref, copies_ref):
    squares = jnp.sum(squares_ref[...], axis=0)
    scale = jnp.minimum(1.0, math.sqrt(D * 2 * KVH * HD) / jnp.sqrt(squares))[:, :1]
    clipped = sum_ref[...] * scale
    one = BETA_ONE * one_ref[...] + (1.0 - BETA_ONE) * clipped
    two = BETA_TWO * two_ref[...] + (1.0 - BETA_TWO) * clipped * clipped
    new_one_ref[...] = one
    new_two_ref[...] = two
    update = one / FIRST_CORR / (jnp.sqrt(two / SECOND_CORR) + EPSILON)
    weights = (master_ref[...] - LEARN_RATE * update).astype(jnp.bfloat16)
    for i in range(copies_ref.shape[0]):
        copies_ref[i] = weights


def cache_kernel(len_ref, q_ref, k_ref, v_ref, qs_ref, acc_ref, max_ref, sum_ref, qf_ref):
    rows, slots = k_ref.shape[0], k_ref.shape[1]
    steps = q_ref.shape[1]
    qf_ref[...] = jnp.zeros_like(qf_ref)
    for r in range(rows):
        q = q_ref[r].astype(jnp.float32)
        for h in range(GROUPS):
            qf_ref[pl.ds(r * QROWS + h * steps, steps), :] = q[:, h * HD : (h + 1) * HD]
    qs_ref[...] = qf_ref[...].astype(jnp.bfloat16)
    slot = lax.broadcasted_iota(jnp.int32, (QROWS, slots), 1)
    for r in range(rows):
        qb = qf_ref[pl.ds(r * QROWS, QROWS), :].astype(jnp.bfloat16)
        s = lax.dot_general(qb, k_ref[r], (((1,), (1,)), ((), ())), preferred_element_type=jnp.float32)
        s = jnp.where(slot < len_ref[r], s * (1.0 / math.sqrt(HD)), NEG_FILL)
        top = jnp.max(s, axis=1, keepdims=True)
        p = jnp.exp(s - top)
        total = jnp.sum(p, axis=1, keepdims=True)
        acc = jnp.dot(p.astype(jnp.bfloat16), v_ref[r], preferred_element_type=jnp.float32)
        at = pl.ds(r * QROWS, QROWS)
        acc_ref[at, :] = acc
        max_ref[at, :] = jnp.broadcast_to(top, (QROWS, HD))
        sum_ref[at, :] = jnp.broadcast_to(total, (QROWS, HD))


def tail_kernel(part_ref, cos_ref, sin_ref, q_ref, acc_ref, max_ref, sum_ref, new_ref, out_ref, o_ref, n_ref):
    tokens = part_ref.shape[1]
    rows, steps = out_ref.shape[0], out_ref.shape[1]
    projected = part_ref[0].astype(jnp.float32)
    for i in range(1, part_ref.shape[0]):
        projected = projected + part_ref[i].astype(jnp.float32)
    k, v = projected[:, :HD], projected[:, HD:]
    turned = pltpu.roll(k, HD // 2, 1)
    k = k * cos_ref[...] + turned * sin_ref[...]
    kb, vb = k.astype(jnp.bfloat16), v.astype(jnp.bfloat16)
    n_ref[:, :HD] = k
    n_ref[:, HD:] = v
    for r in range(rows):
        new_ref[r] = n_ref[pl.ds(r * steps, steps), :].astype(jnp.bfloat16)
    total_q = q_ref.shape[0]
    s = lax.dot_general(q_ref[...], kb, (((1,), (1,)), ((), ())), preferred_element_type=jnp.float32)
    s = s * (1.0 / math.sqrt(HD))
    q_at = lax.broadcasted_iota(jnp.int32, (total_q, tokens), 0)
    t_at = lax.broadcasted_iota(jnp.int32, (total_q, tokens), 1)
    ok = t_at < 0
    for r in range(rows):
        inside = (q_at >= r * QROWS) & (q_at < (r + 1) * QROWS) & (t_at >= r * steps)
        ok = ok | (inside & (t_at <= r * steps + (q_at & (steps - 1))))
    s = jnp.where(ok, s, NEG_FILL)
    top = jnp.maximum(jnp.max(s, axis=1, keepdims=True), max_ref[...])
    p = jnp.where(ok, jnp.exp(s - top[:, :1]), 0.0)
    fade = jnp.exp(max_ref[...] - top)
    total = sum_ref[...] * fade + jnp.sum(p, axis=1, keepdims=True)
    acc = acc_ref[...] * fade + jnp.dot(p.astype(jnp.bfloat16), vb, preferred_element_type=jnp.float32)
    o_ref[...] = acc / total
    for r in range(rows):
        for h in range(GROUPS):
            out_ref[r, :, h * HD : (h + 1) * HD] = o_ref[pl.ds(r * QROWS + h * steps, steps), :].astype(jnp.bfloat16)


VMEM = pl.BlockSpec(memory_space=pltpu.VMEM)
SMEM = pl.BlockSpec(memory_space=pltpu.SMEM)


def body(grad_parts, master, moment_one, moment_two, hidden_in, queries, cache_keys, cache_values, cache_lengths):
    k_rows, col_width = master.shape
    row_count, step_count, model_width = hidden_in.shape
    tokens = row_count * step_count
    n_split = 4 * ZL
    n_tp = 8
    depth = model_width // n_split
    all_q = row_count * QROWS

    tiles = jnp.moveaxis(grad_parts[0].reshape(k_rows, n_tp, col_width), 1, 0)
    arrived = swapped(tiles, TP)
    grad_sum, blocks = pl.pallas_call(
        norm_kernel,
        out_shape=(
            jax.ShapeDtypeStruct((k_rows, col_width), jnp.float32),
            jax.ShapeDtypeStruct((n_split * 2, tokens // 2, depth + 64), jnp.bfloat16),
        ),
        in_specs=[VMEM] * 2,
        out_specs=(VMEM,) * 2,
        scratch_shapes=[pltpu.VMEM((tokens // 2, model_width), jnp.float32)],
    )(near(arrived), near(hidden_in))
    blocks = swapped(blocks, SPLIT + ("c",), [SPLIT_CORE_ORDER])
    squares = pl.pallas_call(
        functools.partial(share_kernel, depth=depth),
        out_shape=jax.ShapeDtypeStruct((ZH * 4, 1, HD), jnp.float32),
        in_specs=[VMEM],
        out_specs=VMEM,
    )(near(blocks))
    blocks, squares, cache_lengths = lax.optimization_barrier((blocks, squares, cache_lengths))
    inputs = blocks[:, :, :depth].reshape(n_split * tokens, depth)
    squares = swapped(squares, ("zh", "y"), [NORM_ORDER])

    q_rows, old_acc, old_max, old_sum = pl.pallas_call(
        cache_kernel,
        out_shape=(
            jax.ShapeDtypeStruct((all_q, HD), jnp.bfloat16),
            jax.ShapeDtypeStruct((all_q, HD), jnp.float32),
            jax.ShapeDtypeStruct((all_q, HD), jnp.float32),
            jax.ShapeDtypeStruct((all_q, HD), jnp.float32),
        ),
        in_specs=[SMEM, VMEM, VMEM, VMEM],
        out_specs=(VMEM,) * 4,
        scratch_shapes=[pltpu.VMEM((all_q, HD), jnp.float32)],
    )(cache_lengths, queries, cache_keys, cache_values)

    half = HD // 2
    inverse = jnp.asarray(ROPE_BASE ** (-2.0 * np.arange(half) / HD), jnp.float32)
    positions = (cache_lengths[:, None] + jnp.arange(step_count, dtype=jnp.int32)[None, :]).astype(jnp.float32)
    turns = positions.reshape(tokens, 1) * inverse[None, :]
    cosine, sine = jnp.cos(turns), jnp.sin(turns)
    cosine = jnp.concatenate([cosine, cosine], -1)
    sine = jnp.concatenate([-sine, sine], -1)


    square = jax.ShapeDtypeStruct((k_rows, col_width), jnp.float32)
    new_moment_one, new_moment_two, copies = pl.pallas_call(
        update_kernel,
        out_shape=(square, square, jax.ShapeDtypeStruct((ZH, k_rows, col_width), jnp.bfloat16)),
        in_specs=[VMEM] * 5,
        out_specs=(VMEM,) * 3,
    )(near(squares), near(grad_sum), near(master), near(moment_one), near(moment_two))
    rows_here = swapped(copies, ("zh",), [ORDER])
    cached, angles = (q_rows, old_acc, old_max, old_sum), (cosine, sine)
    rows_here, inputs, cached, angles = lax.optimization_barrier((rows_here, inputs, cached, angles))
    shares = jnp.dot(inputs, rows_here.reshape(ZH * k_rows, col_width), preferred_element_type=jnp.float32)
    parts = swapped(shares.reshape(n_split, tokens, col_width), SPLIT, [SPLIT_ORDER])

    entries, attended = pl.pallas_call(
        tail_kernel,
        out_shape=(
            jax.ShapeDtypeStruct((row_count, step_count, col_width), jnp.bfloat16),
            jax.ShapeDtypeStruct((row_count, step_count, GROUPS * HD), jnp.bfloat16),
        ),
        in_specs=[VMEM] * 7,
        out_specs=(VMEM,) * 2,
        scratch_shapes=[pltpu.VMEM((all_q, HD), jnp.float32), pltpu.VMEM((tokens, col_width), jnp.float32)],
    )(*[near(array) for array in (parts, *angles, *cached)])
    return (new_moment_one, new_moment_two, entries, attended)


def solution(mesh):
    torus = Mesh(mesh.devices.reshape(2, ZH, ZL, 2, 4, 2), ("g", "zh", "zl", "xl", "y", "c"))
    return jax.shard_map(
        body,
        mesh=torus,
        in_specs=(
            P(TP, GRP_REP, None),
            P(GRP_REP, TP),
            P(GRP_REP, TP),
            P(GRP_REP, TP),
            P(GRP_REP, None, None),
            P(GRP_REP, None, TP),
            P(GRP_REP, None, TP),
            P(GRP_REP, None, TP),
            P(GRP_REP),
        ),
        out_specs=(P(GRP_REP, TP), P(GRP_REP, TP), P(GRP_REP, None, TP), P(GRP_REP, None, TP)),
        check_vma=False,
    )
```
